512 devices in a mesh: ens: 2 (over core), lat: 32 (over z, x), chan: 8 (over y).
Axes of the slice: x: 4, y: 8, z: 8, core: 2. Of those that a mesh axis runs over, the one named last changes fastest.
Arguments:
- field: bfloat16 [2, 384, 128, 256], P('ens', 'chan', 'lat'), may hold values from -6 to 6
- cotangent: bfloat16 [2, 384, 128, 256], P('ens', 'chan', 'lat'), may hold values from -6 to 6
- spec_weight: float32 [2, 64, 384], P(None, None, 'chan'), may hold values from -8 to 8
- disco_coef: float32 [128, 9], replicated, may hold values from -2 to 2
- disco_weight: float32 [9, 384], P(None, 'chan'), may hold values from -5 to 5
- disco_rows: int32 [128, 9], replicated, may hold values from 0 to 127, as said below
- disco_shift: int32 [128, 9], replicated, may hold values from -8 to 8
- w_hidden: bfloat16 [384, 768], replicated, may hold values from -0.3125 to 0.3125
- w_output: bfloat16 [768, 384], replicated, may hold values from -0.21875 to 0.21875
Outputs:
- grad_field: bfloat16 [2, 384, 128, 256], P('ens', 'chan', 'lat')
- grad_spec_weight: float32 [2, 64, 384], P(None, None, 'chan')
- grad_disco_weight: float32 [9, 384], P(None, 'chan')
- grad_w_hidden: float32 [384, 768], P('lat')
- grad_w_output: float32 [768, 384], P('lat')
The draws below stay inside these ranges and needn't reach their ends.
Inputs may be any that keep to these rules, and one draw needn't show every extreme that they name: Entry k of row i of disco_rows names a latitude row within 2 rows of i.
All inputs are finite; a program needn't handle non-finite values.
Results may differ from the reference program's by a relative error of at most 0.013.
Values may be sent and summed in bfloat16 or wider, within the bound.
A program may use at most 64 MiB of HBM per device.

```python
import math
import jax
import jax.numpy as jnp
from jax import lax

C = 384
HID = 768
KS = 9
HALO = 2
SHIFT = 8
NLAT = 128
NLON = 256
MMAX = 64
LMAX = 64
ENS = 2


def draw_disco_rows(key, part):
    centre = jnp.arange(NLAT, dtype=jnp.int32)[:, None]
    offsets = jax.random.randint(key, (NLAT, KS), -HALO, HALO + 1, dtype=jnp.int32)
    column = jnp.arange(KS, dtype=jnp.int32)[None, :]
    offsets = jnp.where(column == 0, -HALO, jnp.where(column == 1, HALO, offsets))
    return jnp.clip(centre + offsets, 0, NLAT - 1).astype(jnp.int32)


def with_ends(entries, own_key, least, high):
    longest = entries.shape.index(max(entries.shape))
    spots = []
    for shift in (0, 1):
        where = [jax.random.randint(jax.random.fold_in(own_key, axis), (), 0, length) for axis, length in enumerate(entries.shape)]
        where[longest] = (where[longest] + shift) % entries.shape[longest]
        spots.append(tuple(where))
    return entries.at[spots[0]].set(least).at[spots[1]].set(high)


def steps_of(own_key, shape, cuts, low, largest):
    loudness = 1.0
    for axis_at, parts in cuts:
        steps = jax.random.uniform(jax.random.fold_in(jax.random.fold_in(own_key, 6), axis_at), (parts,), jnp.float32, low / len(cuts), largest / len(cuts))
        loudness = loudness * jnp.repeat(jnp.exp(steps), shape[axis_at] // parts).reshape((-1,) + (1,) * (len(shape) - 1 - axis_at))
    return loudness


def normal_values(rng, extent, deviation, limit, cuts=(), kind=jnp.bfloat16):
    loudness = steps_of(rng, extent, cuts, -0.22, 0.18) if cuts else 1.0
    entries = jax.random.normal(rng, extent, jnp.float32) * deviation * loudness
    return jnp.minimum(jnp.maximum(entries, -limit), limit).astype(kind)


def setup_inputs(seed: int = 0) -> dict:
    seeds = jax.random.split(jax.random.key(seed), 10)
    return {
        "field": normal_values(seeds[0], (ENS, C, NLAT, NLON), 1.0, 6.0, ((0, 2), (1, 8), (2, 32))),
        "cotangent": normal_values(seeds[1], (ENS, C, NLAT, NLON), 1.0, 6.0, ((0, 2), (1, 8), (2, 32))),
        "spec_weight": normal_values(seeds[2], (2, LMAX, C), 2.0, 8.0, ((2, 8),), jnp.float32),
        "disco_coef": normal_values(seeds[3], (NLAT, KS), 0.33, 2.0, (), jnp.float32),
        "disco_weight": normal_values(seeds[4], (KS, C), 1.0, 5.0, ((1, 8),), jnp.float32),
        "disco_rows": draw_disco_rows(jax.random.fold_in(seeds[9], 71), 0),
        "disco_shift": with_ends(jax.random.randint(seeds[6], (NLAT, KS), 0 - SHIFT, SHIFT + 1), jax.random.fold_in(seeds[6], 1), 0 - SHIFT, SHIFT).astype(jnp.int32),
        "w_hidden": normal_values(seeds[7], (C, HID), C ** -0.5, 0.3125),
        "w_output": normal_values(seeds[8], (HID, C), HID ** -0.5, 0.21875),
    }


norm_eps = 1e-06
inv_root_two = 0.7071067811865476
inv_root_tau = 0.3989422804014327
highest = lax.Precision.HIGHEST

def colatitudes(lat_count):
    return (jnp.arange(lat_count, dtype=jnp.int32).astype(jnp.float32) + 0.5) * (math.pi / lat_count)

def legendre_rows(first_order, order_count, lat_count, degree_count, unrolled):
    colatitude = colatitudes(lat_count)
    cosine = jnp.cos(colatitude)
    sine_rows = jnp.sin(colatitude)
    orders = (first_order + jnp.arange(order_count, dtype=jnp.int32)).astype(jnp.float32)
    log_start = 0.5 * (jnp.log((2.0 * orders + 1.0) / (4.0 * math.pi)) + lax.lgamma(orders + 0.5) - lax.lgamma(orders + 1.0) - 0.5 * math.log(math.pi))
    diagonal = jnp.exp(log_start[:, None] + orders[:, None] * jnp.log(sine_rows)[None, :])

    def advance(carry, degree):
        previous, before = carry
        degree_value = degree.astype(jnp.float32)
        above = degree_value > orders
        upper_term = jnp.where(above, 4.0 * degree_value * degree_value - 1.0, 1.0)
        lower_term = jnp.where(above, degree_value * degree_value - orders * orders, 1.0)
        factor = jnp.sqrt(upper_term / lower_term)
        behind = jnp.where(above, (degree_value - 1.0) * (degree_value - 1.0) - orders * orders, 0.0)
        damping = jnp.sqrt(behind / (4.0 * (degree_value - 1.0) * (degree_value - 1.0) - 1.0))
        recurred = factor[:, None] * (cosine[None, :] * previous - damping[:, None] * before)
        current = jnp.where(above[:, None], recurred, jnp.where((degree_value == orders)[:, None], diagonal, 0.0))
        return ((current, previous), current)
    zero_rows = jnp.zeros((order_count, lat_count), jnp.float32)
    finish, stacked = lax.scan(advance, (zero_rows, zero_rows), jnp.arange(degree_count, dtype=jnp.int32), unroll=unrolled)
    return jnp.transpose(stacked, (1, 0, 2))

def quadrature(lat_count, lon_count):
    return 2.0 * math.pi / lon_count * (math.pi / lat_count) * jnp.sin(colatitudes(lat_count))

def lon_tables(lon_count, mode_count):
    columns = jnp.arange(lon_count, dtype=jnp.int32)
    mode_ids = jnp.arange(mode_count, dtype=jnp.int32)
    phase_ids = columns[:, None] * mode_ids[None, :] % lon_count
    angles = phase_ids.astype(jnp.float32) * (2.0 * math.pi / lon_count)
    cosine = jnp.cos(angles)
    sine_part = jnp.sin(angles)
    forward = jnp.concatenate([cosine, -sine_part], axis=1).astype(jnp.bfloat16)
    doubled = jnp.where(mode_ids == 0, 1.0, 2.0).astype(jnp.float32)[None, :]
    inverse = jnp.transpose(jnp.concatenate([doubled * cosine, -doubled * sine_part], axis=1)).astype(jnp.bfloat16)
    return (forward, inverse)

def apply_filter(coeffs, spec_weight):
    real_weight = jnp.transpose(spec_weight[0])[:, None, :]
    imag_weight = jnp.transpose(spec_weight[1])[:, None, :]
    real_part = coeffs[:, 0]
    imag_part = coeffs[:, 1]
    return jnp.stack([real_weight * real_part - imag_weight * imag_part, real_weight * imag_part + imag_weight * real_part], axis=1)

def filter_adjoint(grads, coeffs, spec_weight):
    real_weight = jnp.transpose(spec_weight[0])[:, None, :]
    imag_weight = jnp.transpose(spec_weight[1])[:, None, :]
    grad_real = grads[:, 0]
    grad_imag = grads[:, 1]
    real_part = coeffs[:, 0]
    imag_part = coeffs[:, 1]
    weight_zero = jnp.transpose(lax.optimization_barrier(jnp.sum(grad_real * real_part + grad_imag * imag_part, axis=1)))
    weight_one = jnp.transpose(lax.optimization_barrier(jnp.sum(grad_imag * real_part - grad_real * imag_part, axis=1)))
    adjoint_coeffs = jnp.stack([real_weight * grad_real + imag_weight * grad_imag, real_weight * grad_imag - imag_weight * grad_real], axis=1)
    return (adjoint_coeffs, jnp.stack([weight_zero, weight_one], axis=0))

def mlp_backward(mixed_rows, adjoint_rows, w_hidden, w_output):
    mixed32 = mixed_rows.astype(jnp.float32)
    rscale = lax.rsqrt(lax.optimization_barrier(jnp.mean(mixed32 * mixed32, axis=0, keepdims=True)) + norm_eps)
    normed32 = mixed32 * rscale
    normed = normed32.astype(jnp.bfloat16)
    preact = lax.dot_general(w_hidden, normed, (((0,), (0,)), ((), ())), preferred_element_type=jnp.float32)
    activated = jax.nn.gelu(preact, approximate=False).astype(jnp.bfloat16)
    grad_output = lax.dot_general(activated, adjoint_rows, (((1,), (1,)), ((), ())), preferred_element_type=jnp.float32)
    grad_act = lax.dot_general(w_output, adjoint_rows, (((1,), (0,)), ((), ())), preferred_element_type=jnp.float32)
    cumulative = 0.5 * (1.0 + lax.erf(preact * inv_root_two))
    density = jnp.exp(-0.5 * preact * preact) * inv_root_tau
    grad_pre = (grad_act * (cumulative + preact * density)).astype(jnp.bfloat16)
    grad_hidden = lax.dot_general(normed, grad_pre, (((1,), (1,)), ((), ())), preferred_element_type=jnp.float32)
    grad_normed = lax.dot_general(w_hidden, grad_pre, (((1,), (0,)), ((), ())), preferred_element_type=jnp.float32)
    grad_mixed = (rscale * (grad_normed - normed32 * lax.optimization_barrier(jnp.mean(grad_normed * normed32, axis=0, keepdims=True)))).astype(jnp.bfloat16)
    return (grad_mixed, grad_hidden, grad_output)

def reference(field, cotangent, spec_weight, disco_coef, disco_weight, disco_rows, disco_shift, w_hidden, w_output):
    forward, inverse = lon_tables(NLON, MMAX)
    legendre = legendre_rows(0, MMAX, NLAT, LMAX, 1)
    weighted = legendre * quadrature(NLAT, NLON)[None, None, :]
    grad_scale = 1.0 / math.sqrt(ENS * NLAT * NLON)
    columns = jnp.arange(NLON, dtype=jnp.int32)
    lat_ids = jnp.arange(NLAT, dtype=jnp.int32)
    sum_hidden = jnp.zeros((C, HID), jnp.float32)
    sum_output = jnp.zeros((HID, C), jnp.float32)
    sum_filter = jnp.zeros((2, LMAX, C), jnp.float32)
    sum_disco = jnp.zeros((KS, C), jnp.float32)
    results = []
    for member_id in range(ENS):
        member = field[member_id]
        adjoint_member = cotangent[member_id]
        spectrum = jnp.dot(member.reshape(C * NLAT, NLON), forward, preferred_element_type=jnp.float32)
        spectrum = spectrum.astype(jnp.bfloat16).reshape(C, NLAT, 2, MMAX)
        coeffs = jnp.einsum('citm,mli->ctml', spectrum.astype(jnp.float32), weighted, precision=highest)
        synth = jnp.einsum('ctml,mli->citm', apply_filter(coeffs, spec_weight), legendre, precision=highest).astype(jnp.bfloat16)
        spectral = jnp.dot(synth.reshape(C * NLAT, 2 * MMAX), inverse, preferred_element_type=jnp.float32).reshape(C, NLAT, NLON)
        disco_out = jnp.zeros((C, NLAT, NLON), jnp.float32)
        for entry in range(KS):
            lon_index = (columns[None, :] + disco_shift[:, entry][:, None]) % NLON
            shifted = member[:, disco_rows[:, entry][:, None], lon_index]
            mixing = disco_coef[:, entry][None, :, None] * disco_weight[entry][:, None, None]
            disco_out = disco_out + shifted.astype(jnp.float32) * mixing
        mixed_field = (spectral + disco_out).astype(jnp.bfloat16)

        def mlp_step(carry, pair):
            total_hidden, total_output = carry
            grad_row, part_hidden, part_output = mlp_backward(pair[0], pair[1], w_hidden, w_output)
            return ((total_hidden + part_hidden, total_output + part_output), grad_row)
        totals, grad_rows = lax.scan(mlp_step, (sum_hidden, sum_output), (jnp.moveaxis(mixed_field, 1, 0), jnp.moveaxis(adjoint_member, 1, 0)))
        sum_hidden, sum_output = totals
        grad_mixed = jnp.moveaxis(grad_rows, 0, 1)
        grad_synth = lax.dot_general(grad_mixed.reshape(C * NLAT, NLON), inverse, (((1,), (1,)), ((), ())), preferred_element_type=jnp.float32)
        grad_synth = grad_synth.astype(jnp.bfloat16).reshape(C, NLAT, 2, MMAX)
        grad_filtered = jnp.einsum('citm,mli->ctml', grad_synth.astype(jnp.float32), legendre, precision=highest)
        grad_coeffs, filter_part = filter_adjoint(grad_filtered, coeffs, spec_weight)
        sum_filter = sum_filter + filter_part
        grad_spectrum = jnp.einsum('ctml,mli->citm', grad_coeffs, weighted, precision=highest).astype(jnp.bfloat16)
        spectral_back = lax.dot_general(grad_spectrum.reshape(C * NLAT, 2 * MMAX), forward, (((1,), (1,)), ((), ())), preferred_element_type=jnp.float32).reshape(C, NLAT, NLON)
        grad_mixed32 = grad_mixed.astype(jnp.float32)
        spread = jnp.zeros((C, NLAT, NLON), jnp.float32)
        for entry in range(KS):
            lon_index = (columns[None, :] + disco_shift[:, entry][:, None]) % NLON
            shifted = member[:, disco_rows[:, entry][:, None], lon_index]
            inner_sum = lax.optimization_barrier(jnp.sum(shifted.astype(jnp.float32) * grad_mixed32, axis=2))
            sum_disco = sum_disco.at[entry].add(lax.optimization_barrier(jnp.sum(inner_sum * disco_coef[:, entry][None, :], axis=1)))
            mixing = disco_coef[:, entry][None, :, None] * disco_weight[entry][:, None, None]
            contrib = grad_mixed32 * mixing
            back_index = (columns[None, :] - disco_shift[:, entry][:, None]) % NLON
            moved = contrib[:, lat_ids[:, None], back_index]
            spread = spread.at[:, disco_rows[:, entry], :].add(moved)
        results.append((adjoint_member.astype(jnp.float32) + spectral_back + spread).astype(jnp.bfloat16))
    grad_field = jnp.stack(results, axis=0)
    return (grad_field, sum_filter, sum_disco * grad_scale, sum_hidden * grad_scale, sum_output * grad_scale)
```

```python
import functools
import math

import jax
import jax.numpy as jnp
import ml_dtypes
import numpy as np
from jax import lax
from jax.experimental import pallas as pl
from jax.experimental.pallas import tpu as pltpu
from jax.sharding import PartitionSpec as P

MESH = pl.DeviceIdType.MESH
HALO = 2
LANES = 128
norm_eps = 1e-06
inv_root_two = 0.7071067811865476
inv_root_tau = 0.3989422804014327
f32 = jnp.float32
bf16 = jnp.bfloat16
NT = (((1,), (1,)), ((), ()))


def legendre_table(lat_count, order_count, degree_count):
    theta = math.pi * (np.arange(lat_count) + 0.5) / lat_count
    cosine, sine = np.cos(theta), np.sin(theta)
    table = np.zeros((order_count, degree_count, lat_count))
    for m in range(order_count):
        start = 0.5 * (
            math.log((2 * m + 1) / (4 * math.pi))
            + math.lgamma(m + 0.5)
            - math.lgamma(m + 1)
            - math.lgamma(0.5)
        )
        if m < degree_count:
            table[m, m] = np.exp(start + m * np.log(sine))
        for l in range(m + 1, degree_count):
            a = math.sqrt((4 * l * l - 1) / (l * l - m * m))
            b = math.sqrt(((l - 1) ** 2 - m * m) / (4 * (l - 1) ** 2 - 1))
            before = table[m, l - 2] if l >= 2 else 0.0
            table[m, l] = a * (cosine * table[m, l - 1] - b * before)
    return table


def constant_tables(lat_count, lon_count, mode_count, degree_count, bands):
    legendre = legendre_table(lat_count, mode_count, degree_count)
    sine = np.sin(math.pi * (np.arange(lat_count) + 0.5) / lat_count)
    quadrature = (2 * math.pi / lon_count) * (math.pi / lat_count) * sine
    here = mode_count // bands
    shape = (bands, here * degree_count, lat_count)
    plain = legendre.reshape(shape).astype(np.float32).astype(ml_dtypes.bfloat16)
    weighted = (legendre * quadrature).reshape(shape).astype(np.float32).astype(ml_dtypes.bfloat16)
    modes = np.arange(mode_count)
    phase = 2 * math.pi * ((modes[:, None] * np.arange(lon_count)[None, :]) % lon_count) / lon_count
    scale = np.where(modes == 0, 1.0, 2.0)[:, None]
    cos_rows = np.cos(phase).reshape(bands, 1, here, lon_count)
    sin_rows = -np.sin(phase).reshape(bands, 1, here, lon_count)
    forward = np.concatenate([cos_rows, sin_rows], axis=1).reshape(2 * mode_count, lon_count)
    doubled = np.repeat(scale.reshape(bands, 1, here, 1), 2, axis=1).reshape(2 * mode_count, 1)
    cast = lambda v: v.astype(np.float32).astype(ml_dtypes.bfloat16)
    return plain, weighted, cast(forward), cast(forward * doubled)


class Names:
    def __init__(self, names, refs):
        for name, ref in zip(names, refs, strict=True):
            setattr(self, name, ref)


ARGS = (
    "field", "cot", "sw", "dw", "wh", "wo", "fwd", "inv", "coef", "rows", "shift", "p_hbm",
    "q_hbm", "gfield", "gsw", "gdw", "gh", "go",
)
DMAS = (
    "a1", "a2", "cot", "mix", "grd", "a5", "a6", "lo", "hi", "glo", "ghi", "re", "fa", "fb", "fc",
    "ra0", "ra1", "ra2", "rb0", "rb1", "rb2", "rc0", "rc1", "rc2", "rd0", "rd1", "rd2",
)
S = {name: i for i, name in enumerate(DMAS)}


def scratch(n):
    piece = n.qn * n.rows
    return dict(
        pt=pltpu.VMEM((n.ml * n.deg, n.lat), bf16),
        qt=pltpu.VMEM((n.ml * n.deg, n.lat), bf16),
        qa=pltpu.VMEM((n.qn * n.deg, n.nb * piece), bf16),
        pa=pltpu.VMEM((n.qn * n.deg, n.nb * piece), bf16),
        qb=pltpu.VMEM((n.nb * piece, n.qn * n.deg), bf16),
        pb=pltpu.VMEM((n.nb * piece, n.qn * n.deg), bf16),
        wht=pltpu.VMEM((n.hid, n.chans), bf16),
        spread_rows=pltpu.VMEM((n.nb * piece, LANES), f32),
        s1=pltpu.VMEM((n.nb, piece, LANES), bf16),
        r1=pltpu.VMEM((n.nb, piece, LANES), bf16),
        s2=pltpu.VMEM((n.nb, piece, LANES), bf16),
        r2=pltpu.VMEM((n.nb, piece, LANES), bf16),
        s5=pltpu.VMEM((n.nb, piece, LANES), bf16),
        r5=pltpu.VMEM((n.nb, piece, LANES), bf16),
        s6=pltpu.VMEM((n.nb, piece, LANES), bf16),
        r6=pltpu.VMEM((n.nb, piece, LANES), bf16),
        coeffs=pltpu.VMEM((n.qn * n.deg, LANES), f32),
        sww=pltpu.VMEM((2, n.ml * n.deg, LANES), f32),
        halo=pltpu.VMEM((2, HALO, n.cl, n.lon), bf16),
        ghalo=pltpu.VMEM((2, HALO, n.cl, n.lon), bf16),
        fext=pltpu.VMEM((n.rows + 2 * HALO, n.cl, n.lon), f32),
        gm=pltpu.VMEM((n.rows, n.cl, n.lon), bf16),
        shifted=pltpu.VMEM((n.rows * n.ks, n.cl, n.lon), f32),
        square=pltpu.VMEM((LANES, LANES), f32),
        wcol=pltpu.VMEM((n.ks, n.cl, n.lon), f32),
        disco=pltpu.VMEM((n.rows, n.cl, n.lon), f32),
        back=pltpu.VMEM((n.rows, n.cl, n.lon), f32),
        dgrad=pltpu.VMEM((LANES, LANES), f32),
        cotall=pltpu.VMEM((n.ng, n.cl, LANES), bf16),
        mixs=pltpu.VMEM((n.ng, n.cl, LANES), bf16),
        mixall=pltpu.VMEM((n.ng, n.cl, LANES), bf16),
        gact=pltpu.VMEM((n.hid, LANES), f32),
        gpre=pltpu.VMEM((n.hid, LANES), bf16),
        gs=pltpu.VMEM((n.ng, n.cl, LANES), bf16),
        gr=pltpu.VMEM((n.ng, n.cl, LANES), bf16),
        wide=pltpu.VMEM((n.cl, n.rows, n.lon), f32),
        fld=pltpu.VMEM((n.rows, n.cl, n.lon), bf16),
        cot8=pltpu.VMEM((n.ng, n.cl, LANES), bf16),
        n32=pltpu.VMEM((n.chans, LANES), f32),
        np32=pltpu.VMEM((n.chans, LANES), f32),
        ap32=pltpu.VMEM((n.hid, LANES), f32),
        was=pltpu.VMEM((2, n.kc, n.nx, n.hid // n.nx, LANES), bf16),
        war=pltpu.VMEM((n.kc, n.nx, n.hid // n.nx, LANES), bf16),
        wbs=pltpu.VMEM((n.kc, n.nx, n.hid // n.nx, LANES), bf16),
        wbr=pltpu.VMEM((n.kc, n.nx, n.hid // n.nx, LANES), bf16),
        wsum=pltpu.VMEM((n.hid // n.nx, LANES), f32),
        wslot=pltpu.VMEM((n.nz, n.slot, LANES), f32),
        wcs=pltpu.VMEM((n.kc, n.nz, n.slot, LANES), bf16),
        wcr=pltpu.VMEM((n.kc, n.nz, n.slot, LANES), bf16),
        wds=pltpu.VMEM((n.kc, n.slot, LANES), bf16),
        wdr=pltpu.VMEM((n.kc, n.ng, n.slot, LANES), bf16),
        wtot=pltpu.VMEM((2, n.kc, n.slot, LANES), f32),
        fas=pltpu.VMEM((n.nx, 2 * n.frows, LANES), bf16),
        far=pltpu.VMEM((n.nx, 2 * n.frows, LANES), bf16),
        fbs=pltpu.VMEM((2 * n.frows, LANES), bf16),
        fbr=pltpu.VMEM((2 * n.nz, 2 * n.frows, LANES), bf16),
        fcr=pltpu.VMEM((n.nx, n.frows, LANES), f32),
        load_sem=pltpu.SemaphoreType.DMA((2,)),
        send=pltpu.SemaphoreType.DMA((len(DMAS),)),
        recv=pltpu.SemaphoreType.DMA((len(DMAS),)),
    )


def kernel(n, names, *refs):
    v = Names(list(names), refs)
    me_e, me_b, me_g = (lax.axis_index(a) for a in ("ens", "lat", "chan"))
    me_z, me_x = lax.div(me_b, n.nx), lax.rem(me_b, n.nx)
    first = me_b * n.rows
    piece = n.qn * n.rows
    total_rows = n.nb * piece

    def copy(phase, src, dst, device):
        return pltpu.make_async_remote_copy(
            src_ref=src,
            dst_ref=dst,
            send_sem=v.send.at[S[phase]],
            recv_sem=v.recv.at[S[phase]],
            device_id=device,
            device_id_type=MESH,
        )

    def arrived(phase, ref):
        pltpu.make_async_copy(ref, ref, v.recv.at[S[phase]]).wait()

    def left(phase, ref):
        pltpu.make_async_copy(ref, ref, v.send.at[S[phase]]).wait()

    def lat_peer(k):
        return lax.rem(me_b + k, n.nb)

    def lat_at(t):
        u = lax.div(t, n.nx)
        far = n.nz // 2
        dz = jnp.where(lax.rem(u, 2) == 0, far - lax.div(u, 2), far + lax.div(u + 1, 2))
        dx = lax.rem(n.nx // 2 + n.nx - lax.rem(t, n.nx), n.nx)
        dx = jnp.where(u == n.nz - 1, n.nx // 2 + lax.rem(t, n.nx) - 1, dx)
        return lax.rem(me_z + n.nz + dz, n.nz) * n.nx + lax.rem(me_x + n.nx + dx, n.nx)

    def exchange(phase, axis, me, count, src, dst, whole=False):
        def step(k, carry):
            d = lax.rem(me + k, count)
            copy(phase, src if whole else src.at[d], dst.at[me], {axis: d}).start()
            return carry

        def to_lat(t, carry):
            d = lat_at(t)
            copy(phase, src.at[d], dst.at[me], {axis: d}).start()
            return carry

        if axis == "lat":
            lax.fori_loop(0, count - 1, to_lat, 0)
        else:
            lax.fori_loop(1, count, step, 0)
        dst[me] = src[...] if whole else src[me]

    barrier = pltpu.get_barrier_semaphore()

    def greet(device):
        pl.semaphore_signal(barrier, inc=1, device_id=device, device_id_type=MESH)

    def greet_lat(k, carry):
        greet({"lat": lat_at(k)})
        return carry

    def greet_chan(k, carry):
        greet({"chan": lax.rem(me_g + k, n.ng)})
        return carry

    def greet_ens(k, carry):
        greet({"ens": 1 - me_e, "lat": k * n.nx + me_x})
        return carry

    lax.fori_loop(0, n.nb - 1, greet_lat, 0)
    lax.fori_loop(1, n.ng, greet_chan, 0)
    lax.fori_loop(0, n.nz, greet_ens, 0)

    load_p = pltpu.make_async_copy(v.p_hbm.at[me_b], v.pt, v.load_sem.at[0])
    load_q = pltpu.make_async_copy(v.q_hbm.at[me_b], v.qt, v.load_sem.at[1])
    load_p.start()
    load_q.start()

    def to_pieces(table, row_of, out):
        for r in range(n.rows):
            part = lax.dot_general(table[...], row_of(r), NT, preferred_element_type=f32)
            v.spread_rows[pl.ds(r, 2 * n.modes, stride=n.rows), :] = jnp.concatenate(
                [part, jnp.zeros((2 * n.modes, LANES - n.cl), f32)], axis=1
            )
        out[...] = v.spread_rows[...].astype(bf16).reshape(n.nb, piece, LANES)

    def from_pieces(table, pieces):
        v.spread_rows[...] = pieces[...].reshape(total_rows, LANES).astype(f32)
        rows = []
        for r in range(n.rows):
            part = v.spread_rows[pl.ds(r, 2 * n.modes, stride=n.rows), :]
            flipped = jnp.transpose(part).astype(bf16)[: n.cl]
            rows.append(jnp.dot(flipped, table[...], preferred_element_type=f32))
        return rows

    v.wide[...] = v.field[...].astype(f32)
    for r in range(n.rows):
        row = v.wide[:, r, :]
        v.fext[HALO + r] = row
        v.fld[r] = row.astype(bf16)
    to_pieces(v.fwd, lambda r: v.fld[r], v.s1)
    v.wide[...] = v.cot[...].astype(f32)
    for r in range(n.rows):
        row = v.wide[:, r, :].astype(bf16)
        v.cot8[2 * r] = row[:, :LANES]
        v.cot8[2 * r + 1] = row[:, LANES:]
    pl.semaphore_wait(barrier, n.nb - 1 + n.ng - 1 + n.nz)

    exchange("a1", "lat", me_b, n.nb, v.s1, v.r1)
    below, above = lat_peer(n.nb - 1), lat_peer(1)
    top, bottom = pl.ds(0, HALO), pl.ds(n.rows - HALO, HALO)
    copy("hi", v.fld.at[top], v.halo.at[1], {"lat": below}).start()
    copy("lo", v.fld.at[bottom], v.halo.at[0], {"lat": above}).start()
    exchange("cot", "chan", me_g, n.ng, v.cot8, v.cotall)

    load_p.wait()
    load_q.wait()

    half = n.ml * n.deg
    wide = (n.lat, total_rows)
    column = lax.broadcasted_iota(jnp.int32, wide, 1)
    row_id = lax.broadcasted_iota(jnp.int32, wide, 0)
    lat_of = lax.div(column, piece) * n.rows + lax.rem(column, n.rows)
    expand = jnp.where(lat_of == row_id, 1.0, 0.0).astype(bf16)
    q_of = lax.div(lax.rem(lax.broadcasted_iota(jnp.int32, (half, total_rows), 1), piece), n.rows)
    ml_of = lax.div(lax.broadcasted_iota(jnp.int32, (half, total_rows), 0), n.deg)

    def expanded(table, out):
        both = jnp.dot(table[...], expand, preferred_element_type=f32)
        for t in range(2):
            keep = q_of == ml_of + t * n.ml
            out[t * half : (t + 1) * half, :] = jnp.where(keep, both, 0.0).astype(bf16)

    expanded(v.qt, v.qa)
    expanded(v.pt, v.pa)
    for t in range(2):
        mine = slice(t * half, (t + 1) * half)
        v.pb[:, mine] = jnp.transpose(v.pa[mine, :].astype(f32)).astype(bf16)
    v.square[...] = jnp.zeros((LANES, LANES), f32)
    for t in range(2):
        v.square[: n.cl, : n.deg] = v.sw[t]
        block = jnp.transpose(v.square[...])[: n.deg]
        for m in range(n.ml):
            v.sww[t, m * n.deg : (m + 1) * n.deg, :] = block

    arrived("a1", v.r1.at[pl.ds(0, n.nb - 1)])
    spectrum = v.r1[...].reshape(total_rows, LANES)
    coeffs = jnp.dot(v.qa[...], spectrum, preferred_element_type=f32)
    v.coeffs[...] = coeffs
    real, imag = coeffs[:half], coeffs[half:]
    s0, s1 = v.sww[0], v.sww[1]
    filtered = jnp.concatenate([s0 * real - s1 * imag, s0 * imag + s1 * real], axis=0)
    synth = jnp.dot(v.pb[...], filtered.astype(bf16), preferred_element_type=f32)
    v.s2[...] = synth.astype(bf16).reshape(n.nb, piece, LANES)
    exchange("a2", "lat", me_b, n.nb, v.s2, v.r2)

    v.square[...] = jnp.zeros((LANES, LANES), f32)
    v.square[: n.ks, : n.cl] = v.dw[...]
    columns = jnp.transpose(v.square[...])
    for k in range(n.ks):
        v.wcol[k] = jnp.broadcast_to(columns[: n.cl, k : k + 1], (n.cl, n.lon))
    arrived("lo", v.halo.at[0])
    arrived("hi", v.halo.at[1])
    for r in range(HALO):
        v.fext[r] = v.halo[0, r].astype(f32)
        v.fext[HALO + n.rows + r] = v.halo[1, r].astype(f32)

    for r in range(n.rows):

        def tap(k, total, r=r):
            source = v.rows[k, first + r] - first + HALO
            source = jnp.minimum(jnp.maximum(source, 0), n.rows + 2 * HALO - 1)
            amount = lax.rem(n.lon - v.shift[k, first + r], n.lon)
            moved = pltpu.roll(v.fext[source], amount, 1)
            v.shifted[r * n.ks + k] = moved
            return total + (v.coef[k, first + r] * v.wcol[k]) * moved

        v.disco[r] = lax.fori_loop(0, n.ks, tap, jnp.zeros((n.cl, n.lon), f32))

    for t in range(2):
        mine = slice(t * half, (t + 1) * half)
        v.qb[:, mine] = jnp.transpose(v.qa[mine, :].astype(f32)).astype(bf16)
    v.wht[...] = jnp.transpose(v.wh[...].astype(f32)).astype(bf16)
    arrived("cot", v.cotall.at[pl.ds(0, n.ng - 1)])
    v.gact[...] = jnp.dot(
        v.wo[...], v.cotall[...].reshape(n.chans, LANES), preferred_element_type=f32
    )

    arrived("a2", v.r2.at[pl.ds(0, n.nb - 1)])
    for r, row in enumerate(from_pieces(v.inv, v.r2)):
        mixed = (row + v.disco[r]).astype(bf16)
        v.mixs[2 * r] = mixed[:, :LANES]
        v.mixs[2 * r + 1] = mixed[:, LANES:]
    exchange("mix", "chan", me_g, n.ng, v.mixs, v.mixall)

    arrived("mix", v.mixall.at[pl.ds(0, n.ng - 1)])
    mixed = v.mixall[...].reshape(n.chans, LANES).astype(f32)
    rscale = lax.rsqrt(jnp.sum(mixed * mixed, axis=0, keepdims=True) * (1.0 / n.chans) + norm_eps)
    normed32 = mixed * rscale
    normed = normed32.astype(bf16)
    v.n32[...] = normed32
    preact = jnp.dot(v.wht[...], normed, preferred_element_type=f32)
    cumulative = 0.5 * (1.0 + lax.erf(preact * inv_root_two))
    density = jnp.exp(-0.5 * preact * preact) * inv_root_tau
    activated = preact * cumulative
    grad_pre = (v.gact[...] * (cumulative + preact * density)).astype(bf16)
    v.gpre[...] = grad_pre
    grad_normed = jnp.dot(v.wh[...], grad_pre, preferred_element_type=f32)
    along = jnp.sum(grad_normed * normed32, axis=0, keepdims=True) * (1.0 / n.chans)
    grad_mixed = (rscale * (grad_normed - normed32 * along)).astype(bf16)
    v.gs[...] = grad_mixed.reshape(n.ng, n.cl, LANES)
    exchange("grd", "chan", me_g, n.ng, v.gs, v.gr)

    share = n.chans // n.nb
    for x in range(n.nx):
        for z in range(n.nz):
            at, to = (z * n.nx + x) * share, (x * n.nz + z) * share
            v.np32[to : to + share, :] = v.n32[at : at + share, :]
            v.ap32[2 * to : 2 * (to + share), :] = activated[2 * at : 2 * (at + share)]
    normed = v.np32[...].astype(bf16)
    activated = v.ap32[...].astype(bf16)
    adjoint = v.cotall[...].reshape(n.chans, LANES)
    cols, depth = n.chans // n.nx, n.hid // n.nx

    def r_a(k):
        for half in range(2):
            at = half * n.chans + k * LANES
            hidden = lax.dot_general(
                normed, v.gpre[at : at + LANES, :], NT, preferred_element_type=f32
            ).astype(bf16)
            for x in range(n.nx):
                rows = hidden[x * cols : (x + 1) * cols]
                v.was[0, k, x, half * cols : (half + 1) * cols, :] = rows
        output = lax.dot_general(
            activated, adjoint[k * LANES : (k + 1) * LANES], NT, preferred_element_type=f32
        )
        v.was[1, k] = output.astype(bf16).reshape(n.nx, depth, LANES)
        copy(f"ra{k}", v.was.at[1 - me_e, k], v.war.at[k], {"ens": 1 - me_e}).start()

    def r_b(k):
        arrived(f"ra{k}", v.war.at[k])
        v.wbs[k] = (v.was[me_e, k].astype(f32) + v.war[k].astype(f32)).astype(bf16)

        def send(t, carry):
            x = lax.rem(me_x + t, n.nx)
            copy(f"rb{k}", v.wbs.at[k, x], v.wbr.at[k, me_x], {"lat": me_z * n.nx + x}).start()
            return carry

        lax.fori_loop(1, n.nx, send, 0)
        v.wbr[k, me_x] = v.wbs[k, me_x]

    def r_c(k):
        arrived(f"rb{k}", v.wbr.at[k, pl.ds(0, n.nx - 1)])
        v.wsum[...] = jnp.sum(v.wbr[k].astype(f32), axis=0)

        @pl.when(me_e == 0)
        def _():
            for z in range(n.nz):
                for half in range(2):
                    at, to = half * cols + z * share, half * (n.slot // 2)
                    v.wslot[z, to : to + share, :] = v.wsum[at : at + share, :]

        @pl.when(me_e == 1)
        def _():
            for z in range(n.nz):
                v.wslot[z, : 2 * share, :] = v.wsum[2 * z * share : 2 * (z + 1) * share, :]

        v.wcs[k] = v.wslot[...].astype(bf16)

        def send(t, carry):
            z = lax.rem(me_z + t, n.nz)
            copy(f"rc{k}", v.wcs.at[k, z], v.wcr.at[k, me_z], {"lat": z * n.nx + me_x}).start()
            return carry

        lax.fori_loop(1, n.nz, send, 0)
        v.wcr[k, me_z] = v.wcs[k, me_z]

    def r_d(k):
        arrived(f"rc{k}", v.wcr.at[k, pl.ds(0, n.nz - 1)])
        v.wds[k] = jnp.sum(v.wcr[k].astype(f32), axis=0).astype(bf16)

        def send(t, carry):
            g = lax.rem(me_g + t, n.ng)
            copy(f"rd{k}", v.wds.at[k], v.wdr.at[k, me_g], {"chan": g}).start()
            return carry

        lax.fori_loop(1, n.ng, send, 0)
        v.wdr[k, me_g] = v.wds[k]

    def r_e(k):
        arrived(f"rd{k}", v.wdr.at[k, pl.ds(0, n.ng - 1)])
        v.wtot[me_e, k] = jnp.sum(v.wdr[k].astype(f32), axis=0)

    for k in range(n.kc):
        r_a(k)
    for k in range(n.kc):
        r_b(k)

    arrived("grd", v.gr.at[pl.ds(0, n.ng - 1)])
    for r in range(n.rows):
        v.gm[r] = jnp.concatenate([v.gr[2 * r], v.gr[2 * r + 1]], axis=1)
    to_pieces(v.inv, lambda r: v.gm[r], v.s5)
    exchange("a5", "lat", me_b, n.nb, v.s5, v.r5)
    copy("ghi", v.gm.at[top], v.ghalo.at[1], {"lat": below}).start()
    copy("glo", v.gm.at[bottom], v.ghalo.at[0], {"lat": above}).start()

    lane = lax.broadcasted_iota(jnp.int32, (n.cl, LANES), 1)

    def weight_tap(k, total):
        inner = jnp.zeros((n.cl, n.lon), f32)
        for r in range(n.rows):
            inner = inner + v.coef[k, first + r] * (
                v.shifted[r * n.ks + k] * v.gm[r].astype(f32)
            )
        return total + jnp.where(lane == k, jnp.sum(inner, axis=1, keepdims=True), 0.0)

    weight_grad = lax.fori_loop(0, n.ks, weight_tap, jnp.zeros((n.cl, LANES), f32))
    v.square[...] = jnp.zeros((LANES, LANES), f32)
    v.square[: n.cl, :] = weight_grad
    v.dgrad[...] = jnp.transpose(v.square[...])

    for r in range(n.rows):
        v.back[r] = jnp.zeros((n.cl, n.lon), f32)

    def spread(at, rows_of):
        values = rows_of.astype(f32)
        wanted = first - HALO + at
        held = jnp.minimum(jnp.maximum(wanted, 0), n.lat - 1)
        real_row = jnp.where(held == wanted, 1.0, 0.0).astype(f32)
        targets = [r for r in range(n.rows) if abs(at - HALO - r) <= HALO]

        def tap(k, totals):
            moved = pltpu.roll(values, lax.rem(n.lon + v.shift[k, held], n.lon), 1) * v.wcol[k]
            factor = v.coef[k, held] * real_row
            to = v.rows[k, held]
            return tuple(
                total + jnp.where(to == first + r, factor, 0.0) * moved
                for r, total in zip(targets, totals)
            )

        start = tuple(v.back[r] for r in targets)
        for r, total in zip(targets, lax.fori_loop(0, n.ks, tap, start)):
            v.back[r] = total

    for r in range(n.rows):
        if r == n.rows // 2:
            r_c(0)
        spread(HALO + r, v.gm[r])
    r_c(1)

    arrived("a5", v.r5.at[pl.ds(0, n.nb - 1)])
    grads = jnp.dot(v.pa[...], v.r5[...].reshape(total_rows, LANES), preferred_element_type=f32)
    g_real, g_imag = grads[:half], grads[half:]
    s0, s1 = v.sww[0], v.sww[1]
    g_coeffs = jnp.concatenate([s0 * g_real + s1 * g_imag, s0 * g_imag - s1 * g_real], axis=0)
    back_spec = jnp.dot(v.qb[...], g_coeffs.astype(bf16), preferred_element_type=f32)
    v.s6[...] = back_spec.astype(bf16).reshape(n.nb, piece, LANES)
    exchange("a6", "lat", me_b, n.nb, v.s6, v.r6)

    real, imag = v.coeffs[:half, :], v.coeffs[half:, :]
    terms = (g_real * real + g_imag * imag, g_imag * real - g_real * imag)
    parts = []
    for t in range(2):
        part = terms[t][: n.deg]
        for m in range(1, n.ml):
            part = part + terms[t][m * n.deg : (m + 1) * n.deg]
        parts.append(part)
    low_lanes = lax.broadcasted_iota(jnp.int32, (n.deg, LANES), 1) < 64
    both = jnp.where(low_lanes, parts[0], pltpu.roll(parts[1], 64, 1))
    for x in range(n.nx):
        v.fas[x, : n.frows, :] = both[x * n.frows : (x + 1) * n.frows].astype(bf16)
        v.fas[x, n.frows :, :] = v.dgrad[: n.frows, :].astype(bf16)

    def send_fa(t, carry):
        x = lax.rem(me_x + t, n.nx)
        copy("fa", v.fas.at[x], v.far.at[me_x], {"lat": me_z * n.nx + x}).start()
        return carry

    lax.fori_loop(1, n.nx, send_fa, 0)
    v.far[me_x] = v.fas[me_x]
    r_c(2)

    arrived("glo", v.ghalo.at[0])
    arrived("ghi", v.ghalo.at[1])
    spread(0, v.ghalo[0, 0])
    spread(1, v.ghalo[0, 1])

    place = me_e * n.nz + me_z
    arrived("fa", v.far.at[pl.ds(0, n.nx - 1)])
    v.fbs[...] = jnp.sum(v.far[...].astype(f32), axis=0).astype(bf16)

    def send_fb(t, carry):
        p = lax.rem(place + t, 2 * n.nz)
        to = {"ens": lax.div(p, n.nz), "lat": lax.rem(p, n.nz) * n.nx + me_x}
        copy("fb", v.fbs, v.fbr.at[place], to).start()
        return carry

    lax.fori_loop(1, 2 * n.nz, send_fb, 0)
    v.fbr[place] = v.fbs[...]
    r_d(0)

    spread(HALO + n.rows, v.ghalo[1, 0])
    spread(HALO + n.rows + 1, v.ghalo[1, 1])
    r_d(1)
    r_d(2)

    arrived("a6", v.r6.at[pl.ds(0, n.nb - 1)])
    for r, row in enumerate(from_pieces(v.fwd, v.r6)):
        base = jnp.concatenate([v.cot8[2 * r], v.cot8[2 * r + 1]], axis=1).astype(f32)
        v.wide[:, r, :] = base + row + v.back[r]
    v.gfield[...] = v.wide[...].astype(bf16)

    arrived("fb", v.fbr.at[pl.ds(0, 2 * n.nz - 1)])
    ftot = jnp.sum(v.fbr[...].astype(f32), axis=0)
    v.fcr[me_x] = ftot[: n.frows]

    def send_fc(t, carry):
        x = lax.rem(me_x + t, n.nx)
        copy("fc", v.fcr.at[me_x], v.fcr.at[me_x], {"lat": me_z * n.nx + x}).start()
        return carry

    lax.fori_loop(1, n.nx, send_fc, 0)
    v.gdw[...] = ftot[n.frows : n.frows + n.ks, : n.cl] * n.scale

    for k in range(n.kc):
        r_e(k)
    copy("re", v.wtot.at[me_e], v.wtot.at[me_e], {"ens": 1 - me_e}).start()

    arrived("fc", v.fcr.at[pl.ds(0, n.nx - 1)])
    v.square[: n.deg, :] = v.fcr[...].reshape(n.deg, LANES)
    flipped = jnp.transpose(v.square[...])
    v.gsw[0] = flipped[: n.cl, : n.deg]
    v.gsw[1] = flipped[64 : 64 + n.cl, : n.deg]

    arrived("re", v.wtot.at[0])
    for k in range(n.kc):
        lanes = slice(k * LANES, (k + 1) * LANES)
        upper = slice(n.chans + k * LANES, n.chans + (k + 1) * LANES)
        low = n.slot // 2
        v.gh[:, lanes] = v.wtot[0, k, :share, :] * n.scale
        v.gh[:, upper] = v.wtot[0, k, low : low + share, :] * n.scale
        v.go[:, lanes] = v.wtot[1, k, : 2 * share, :] * n.scale

    for phase, ref in (("a1", v.s1), ("a2", v.s2), ("a5", v.s5), ("a6", v.s6)):
        left(phase, ref.at[pl.ds(0, n.nb - 1)])
    for phase, ref in (("cot", v.cot8), ("mix", v.mixs), ("grd", v.gs)):
        left(phase, ref.at[pl.ds(0, n.ng - 1)])
    left("hi", v.halo.at[1])
    left("lo", v.halo.at[0])
    left("ghi", v.ghalo.at[1])
    left("glo", v.ghalo.at[0])
    for k in range(n.kc):
        left(f"ra{k}", v.war.at[k])
        left(f"rb{k}", v.wbs.at[k, pl.ds(0, n.nx - 1)])
        left(f"rc{k}", v.wcs.at[k, pl.ds(0, n.nz - 1)])
        left(f"rd{k}", v.wdr.at[k, pl.ds(0, n.ng - 1)])
    left("re", v.wtot.at[0])
    left("fa", v.fas.at[pl.ds(0, n.nx - 1)])
    left("fb", v.fbr.at[pl.ds(0, 2 * n.nz - 1)])
    left("fc", v.fcr.at[pl.ds(0, n.nx - 1)])


class Sizes:
    pass


def shards(
    nx,
    field,
    cotangent,
    spec_weight,
    disco_coef,
    disco_weight,
    disco_rows,
    disco_shift,
    w_hidden,
    w_output,
):
    n = Sizes()
    _, n.cl, n.rows, n.lon = field.shape
    n.ne, n.nb, n.ng = (lax.axis_size(a) for a in ("ens", "lat", "chan"))
    n.nx = nx
    n.nz = n.nb // nx
    n.lat = n.rows * n.nb
    n.modes = n.lat // 2
    n.ml = n.modes // n.nb
    n.qn = 2 * n.ml
    n.deg = spec_weight.shape[1]
    n.ks = disco_coef.shape[1]
    n.chans, n.hid = w_hidden.shape
    n.frows = n.deg // n.nx
    n.kc = n.chans // LANES
    n.slot = 2 * (-(-(n.chans // n.nb) // 16) * 16)
    n.scale = 1.0 / math.sqrt(n.ne * n.lat * n.lon)
    plain, weighted, forward, inverse = constant_tables(n.lat, n.lon, n.modes, n.deg, n.nb)
    scratches = scratch(n)
    vmem = pl.BlockSpec(memory_space=pltpu.VMEM)
    smem = pl.BlockSpec(memory_space=pltpu.SMEM)
    hbm = pl.BlockSpec(memory_space=pl.ANY)
    share = n.chans // n.nb
    grad_field, grad_spec, grad_disco, grad_hidden, grad_output = pl.pallas_call(
        functools.partial(kernel, n, ARGS + tuple(scratches)),
        out_shape=(
            jax.ShapeDtypeStruct((n.cl, n.rows, n.lon), bf16),
            jax.ShapeDtypeStruct((2, n.cl, n.deg), f32),
            jax.ShapeDtypeStruct((n.ks, n.cl), f32),
            jax.ShapeDtypeStruct((share, n.hid), f32),
            jax.ShapeDtypeStruct((2 * share, n.chans), f32),
        ),
        in_specs=[vmem] * 8 + [smem] * 3 + [hbm] * 2,
        out_specs=(vmem,) * 5,
        scratch_shapes=list(scratches.values()),
        compiler_params=pltpu.CompilerParams(
            collective_id=0, has_side_effects=True, vmem_limit_bytes=56 * 1024 * 1024
        ),
    )(
        field[0],
        cotangent[0],
        jnp.transpose(spec_weight, (0, 2, 1)),
        disco_weight,
        w_hidden,
        w_output,
        jnp.asarray(forward),
        jnp.asarray(inverse),
        jnp.transpose(disco_coef),
        jnp.transpose(disco_rows),
        jnp.transpose(disco_shift),
        jnp.asarray(plain),
        jnp.asarray(weighted),
    )
    return (
        grad_field[None],
        jnp.transpose(grad_spec, (0, 2, 1)),
        grad_disco,
        grad_hidden,
        grad_output,
    )


def solution(mesh, nx=4):
    in_specs = (
        P("ens", "chan", "lat", None),
        P("ens", "chan", "lat", None),
        P(None, None, "chan"),
        P(),
        P(None, "chan"),
        P(),
        P(),
        P(),
        P(),
    )
    out_specs = (
        P("ens", "chan", "lat", None),
        P(None, None, "chan"),
        P(None, "chan"),
        P("lat", None),
        P("lat", None),
    )
    return jax.shard_map(
        functools.partial(shards, nx),
        mesh=mesh,
        in_specs=in_specs,
        out_specs=out_specs,
        check_vma=False,
    )
```

```python
import functools
import math

import jax
import jax.numpy as jnp
import ml_dtypes
import numpy as np
from jax import lax
from jax.experimental import pallas as pl
from jax.experimental.pallas import tpu as pltpu
from jax.sharding import PartitionSpec as P

MESH = pl.DeviceIdType.MESH
HALO = 2
LANES = 128
norm_eps = 1e-06
inv_root_two = 0.7071067811865476
inv_root_tau = 0.3989422804014327
f32 = jnp.float32
bf16 = jnp.bfloat16
NT = (((1,), (1,)), ((), ()))


def legendre_table(lat_count, order_count, degree_count):
    theta = math.pi * (np.arange(lat_count) + 0.5) / lat_count
    cosine, sine = np.cos(theta), np.sin(theta)
    table = np.zeros((order_count, degree_count, lat_count))
    for m in range(order_count):
        start = 0.5 * (
            math.log((2 * m + 1) / (4 * math.pi))
            + math.lgamma(m + 0.5)
            - math.lgamma(m + 1)
            - math.lgamma(0.5)
        )
        if m < degree_count:
            table[m, m] = np.exp(start + m * np.log(sine))
        for l in range(m + 1, degree_count):
            a = math.sqrt((4 * l * l - 1) / (l * l - m * m))
            b = math.sqrt(((l - 1) ** 2 - m * m) / (4 * (l - 1) ** 2 - 1))
            before = table[m, l - 2] if l >= 2 else 0.0
            table[m, l] = a * (cosine * table[m, l - 1] - b * before)
    return table


def constant_tables(lat_count, lon_count, mode_count, degree_count, bands):
    legendre = legendre_table(lat_count, mode_count, degree_count)
    sine = np.sin(math.pi * (np.arange(lat_count) + 0.5) / lat_count)
    quadrature = (2 * math.pi / lon_count) * (math.pi / lat_count) * sine
    here = mode_count // bands
    shape = (bands, here * degree_count, lat_count)
    plain = legendre.reshape(shape).astype(np.float32).astype(ml_dtypes.bfloat16)
    weighted = (legendre * quadrature).reshape(shape).astype(np.float32).astype(ml_dtypes.bfloat16)
    modes = np.arange(mode_count)
    phase = 2 * math.pi * ((modes[:, None] * np.arange(lon_count)[None, :]) % lon_count) / lon_count
    scale = np.where(modes == 0, 1.0, 2.0)[:, None]
    cos_rows = np.cos(phase).reshape(bands, 1, here, lon_count)
    sin_rows = -np.sin(phase).reshape(bands, 1, here, lon_count)
    forward = np.concatenate([cos_rows, sin_rows], axis=1).reshape(2 * mode_count, lon_count)
    doubled = np.repeat(scale.reshape(bands, 1, here, 1), 2, axis=1).reshape(2 * mode_count, 1)
    cast = lambda v: v.astype(np.float32).astype(ml_dtypes.bfloat16)
    return plain, weighted, cast(forward), cast(forward * doubled)


class Names:
    def __init__(self, names, refs):
        for name, ref in zip(names, refs, strict=True):
            setattr(self, name, ref)


ARGS = (
    "field", "cot", "sw", "dw", "wh", "wo", "fwd", "inv", "coef", "rows", "shift", "p_hbm",
    "q_hbm", "gfield", "gsw", "gdw", "gh", "go",
)
DMAS = (
    "a1", "a2", "cot", "mix", "grd", "a5", "a6", "lo", "hi", "glo", "ghi", "re", "fa", "fb", "fc",
    "ra0", "ra1", "ra2", "rb0", "rb1", "rb2", "rc0", "rc1", "rc2", "rd0", "rd1", "rd2",
)
S = {name: i for i, name in enumerate(DMAS)}


def scratch(n):
    piece = n.qn * n.rows
    return dict(
        pt=pltpu.VMEM((n.ml * n.deg, n.lat), bf16),
        qt=pltpu.VMEM((n.ml * n.deg, n.lat), bf16),
        qa=pltpu.VMEM((n.qn * n.deg, n.nb * piece), bf16),
        pa=pltpu.VMEM((n.qn * n.deg, n.nb * piece), bf16),
        qb=pltpu.VMEM((n.nb * piece, n.qn * n.deg), bf16),
        pb=pltpu.VMEM((n.nb * piece, n.qn * n.deg), bf16),
        wht=pltpu.VMEM((n.hid, n.chans), bf16),
        spread_rows=pltpu.VMEM((n.nb * piece, LANES), f32),
        s1=pltpu.VMEM((n.nb, piece, LANES), bf16),
        r1=pltpu.VMEM((n.nb, piece, LANES), bf16),
        s2=pltpu.VMEM((n.nb, piece, LANES), bf16),
        r2=pltpu.VMEM((n.nb, piece, LANES), bf16),
        s5=pltpu.VMEM((n.nb, piece, LANES), bf16),
        r5=pltpu.VMEM((n.nb, piece, LANES), bf16),
        s6=pltpu.VMEM((n.nb, piece, LANES), bf16),
        r6=pltpu.VMEM((n.nb, piece, LANES), bf16),
        coeffs=pltpu.VMEM((n.qn * n.deg, LANES), f32),
        sww=pltpu.VMEM((2, n.ml * n.deg, LANES), f32),
        halo=pltpu.VMEM((2, HALO, n.cl, n.lon), bf16),
        ghalo=pltpu.VMEM((2, HALO, n.cl, n.lon), bf16),
        fext=pltpu.VMEM((n.rows + 2 * HALO, n.cl, n.lon), f32),
        gm=pltpu.VMEM((n.rows, n.cl, n.lon), bf16),
        shifted=pltpu.VMEM((n.rows * n.ks, n.cl, n.lon), f32),
        square=pltpu.VMEM((LANES, LANES), f32),
        wcol=pltpu.VMEM((n.ks, n.cl, n.lon), f32),
        disco=pltpu.VMEM((n.rows, n.cl, n.lon), f32),
        back=pltpu.VMEM((n.rows, n.cl, n.lon), f32),
        dgrad=pltpu.VMEM((LANES, LANES), f32),
        cotall=pltpu.VMEM((n.ng, n.cl, LANES), bf16),
        mixs=pltpu.VMEM((n.ng, n.cl, LANES), bf16),
        mixall=pltpu.VMEM((n.ng, n.cl, LANES), bf16),
        gact=pltpu.VMEM((n.hid, LANES), f32),
        gpre=pltpu.VMEM((n.hid, LANES), bf16),
        gs=pltpu.VMEM((n.ng, n.cl, LANES), bf16),
        gr=pltpu.VMEM((n.ng, n.cl, LANES), bf16),
        wide=pltpu.VMEM((n.cl, n.rows, n.lon), f32),
        fld=pltpu.VMEM((n.rows, n.cl, n.lon), bf16),
        cot8=pltpu.VMEM((n.ng, n.cl, LANES), bf16),
        n32=pltpu.VMEM((n.chans, LANES), f32),
        np32=pltpu.VMEM((n.chans, LANES), f32),
        ap32=pltpu.VMEM((n.hid, LANES), f32),
        was=pltpu.VMEM((2, n.kc, n.nx, n.hid // n.nx, LANES), bf16),
        war=pltpu.VMEM((n.kc, n.nx, n.hid // n.nx, LANES), bf16),
        wbs=pltpu.VMEM((n.kc, n.nx, n.hid // n.nx, LANES), bf16),
        wbr=pltpu.VMEM((n.kc, n.nx, n.hid // n.nx, LANES), bf16),
        wsum=pltpu.VMEM((n.hid // n.nx, LANES), f32),
        wslot=pltpu.VMEM((n.nz, n.slot, LANES), f32),
        wcs=pltpu.VMEM((n.kc, n.nz, n.slot, LANES), bf16),
        wcr=pltpu.VMEM((n.kc, n.nz, n.slot, LANES), bf16),
        wds=pltpu.VMEM((n.kc, n.slot, LANES), bf16),
        wdr=pltpu.VMEM((n.kc, n.ng, n.slot, LANES), bf16),
        wtot=pltpu.VMEM((2, n.kc, n.slot, LANES), f32),
        fas=pltpu.VMEM((2 * n.nx, n.frows, LANES), bf16),
        far=pltpu.VMEM((2 * n.nx, n.frows, LANES), bf16),
        fbs=pltpu.VMEM((n.frows, LANES), bf16),
        fbr=pltpu.VMEM((n.nz, n.frows, LANES), bf16),
        fcr=pltpu.VMEM((2 * n.nx, n.frows, LANES), f32),
        load_sem=pltpu.SemaphoreType.DMA((2,)),
        send=pltpu.SemaphoreType.DMA((len(DMAS),)),
        recv=pltpu.SemaphoreType.DMA((len(DMAS),)),
    )


def kernel(n, names, *refs):
    v = Names(list(names), refs)
    me_e, me_b, me_g = (lax.axis_index(a) for a in ("ens", "lat", "chan"))
    me_z, me_x = lax.div(me_b, n.nx), lax.rem(me_b, n.nx)
    first = me_b * n.rows
    piece = n.qn * n.rows
    total_rows = n.nb * piece

    def copy(phase, src, dst, device):
        return pltpu.make_async_remote_copy(
            src_ref=src,
            dst_ref=dst,
            send_sem=v.send.at[S[phase]],
            recv_sem=v.recv.at[S[phase]],
            device_id=device,
            device_id_type=MESH,
        )

    def arrived(phase, ref):
        pltpu.make_async_copy(ref, ref, v.recv.at[S[phase]]).wait()

    def left(phase, ref):
        pltpu.make_async_copy(ref, ref, v.send.at[S[phase]]).wait()

    def lat_peer(k):
        return lax.rem(me_b + k, n.nb)

    def lat_at(t):
        u = lax.div(t, n.nx)
        far = n.nz // 2
        dz = jnp.where(lax.rem(u, 2) == 0, far - lax.div(u, 2), far + lax.div(u + 1, 2))
        dx = lax.rem(n.nx // 2 + n.nx - lax.rem(t, n.nx), n.nx)
        dx = jnp.where(u == n.nz - 1, n.nx // 2 + lax.rem(t, n.nx) - 1, dx)
        return lax.rem(me_z + n.nz + dz, n.nz) * n.nx + lax.rem(me_x + n.nx + dx, n.nx)

    def exchange(phase, axis, me, count, src, dst, whole=False):
        def step(k, carry):
            d = lax.rem(me + k, count)
            copy(phase, src if whole else src.at[d], dst.at[me], {axis: d}).start()
            return carry

        def to_lat(t, carry):
            d = lat_at(t)
            copy(phase, src.at[d], dst.at[me], {axis: d}).start()
            return carry

        if axis == "lat":
            lax.fori_loop(0, count - 1, to_lat, 0)
        else:
            lax.fori_loop(1, count, step, 0)
        dst[me] = src[...] if whole else src[me]

    barrier = pltpu.get_barrier_semaphore()

    def greet(device):
        pl.semaphore_signal(barrier, inc=1, device_id=device, device_id_type=MESH)

    def greet_lat(k, carry):
        greet({"lat": lat_at(k)})
        return carry

    def greet_chan(k, carry):
        greet({"chan": lax.rem(me_g + k, n.ng)})
        return carry

    def greet_ens(k, carry):
        greet({"ens": 1 - me_e, "lat": me_z * n.nx + k})
        return carry

    lax.fori_loop(0, n.nb - 1, greet_lat, 0)
    lax.fori_loop(1, n.ng, greet_chan, 0)
    lax.fori_loop(0, n.nx, greet_ens, 0)

    load_p = pltpu.make_async_copy(v.p_hbm.at[me_b], v.pt, v.load_sem.at[0])
    load_q = pltpu.make_async_copy(v.q_hbm.at[me_b], v.qt, v.load_sem.at[1])
    load_p.start()
    load_q.start()

    def to_pieces(table, row_of, out):
        for r in range(n.rows):
            part = lax.dot_general(table[...], row_of(r), NT, preferred_element_type=f32)
            v.spread_rows[pl.ds(r, 2 * n.modes, stride=n.rows), :] = jnp.concatenate(
                [part, jnp.zeros((2 * n.modes, LANES - n.cl), f32)], axis=1
            )
        out[...] = v.spread_rows[...].astype(bf16).reshape(n.nb, piece, LANES)

    def from_pieces(table, pieces):
        v.spread_rows[...] = pieces[...].reshape(total_rows, LANES).astype(f32)
        rows = []
        for r in range(n.rows):
            part = v.spread_rows[pl.ds(r, 2 * n.modes, stride=n.rows), :]
            flipped = jnp.transpose(part).astype(bf16)[: n.cl]
            rows.append(jnp.dot(flipped, table[...], preferred_element_type=f32))
        return rows

    v.wide[...] = v.field[...].astype(f32)
    for r in range(n.rows):
        row = v.wide[:, r, :]
        v.fext[HALO + r] = row
        v.fld[r] = row.astype(bf16)
    to_pieces(v.fwd, lambda r: v.fld[r], v.s1)
    v.wide[...] = v.cot[...].astype(f32)
    for r in range(n.rows):
        row = v.wide[:, r, :].astype(bf16)
        v.cot8[2 * r] = row[:, :LANES]
        v.cot8[2 * r + 1] = row[:, LANES:]
    pl.semaphore_wait(barrier, n.nb - 1 + n.ng - 1 + n.nx)

    exchange("a1", "lat", me_b, n.nb, v.s1, v.r1)
    below, above = lat_peer(n.nb - 1), lat_peer(1)
    top, bottom = pl.ds(0, HALO), pl.ds(n.rows - HALO, HALO)
    copy("hi", v.fld.at[top], v.halo.at[1], {"lat": below}).start()
    copy("lo", v.fld.at[bottom], v.halo.at[0], {"lat": above}).start()
    exchange("cot", "chan", me_g, n.ng, v.cot8, v.cotall)

    load_p.wait()
    load_q.wait()

    half = n.ml * n.deg
    wide = (n.lat, total_rows)
    column = lax.broadcasted_iota(jnp.int32, wide, 1)
    row_id = lax.broadcasted_iota(jnp.int32, wide, 0)
    lat_of = lax.div(column, piece) * n.rows + lax.rem(column, n.rows)
    expand = jnp.where(lat_of == row_id, 1.0, 0.0).astype(bf16)
    q_of = lax.div(lax.rem(lax.broadcasted_iota(jnp.int32, (half, total_rows), 1), piece), n.rows)
    ml_of = lax.div(lax.broadcasted_iota(jnp.int32, (half, total_rows), 0), n.deg)

    def expanded(table, out):
        both = jnp.dot(table[...], expand, preferred_element_type=f32)
        for t in range(2):
            keep = q_of == ml_of + t * n.ml
            out[t * half : (t + 1) * half, :] = jnp.where(keep, both, 0.0).astype(bf16)

    expanded(v.qt, v.qa)
    expanded(v.pt, v.pa)
    for t in range(2):
        mine = slice(t * half, (t + 1) * half)
        v.pb[:, mine] = jnp.transpose(v.pa[mine, :].astype(f32)).astype(bf16)
    v.square[...] = jnp.zeros((LANES, LANES), f32)
    for t in range(2):
        v.square[: n.cl, : n.deg] = v.sw[t]
        block = jnp.transpose(v.square[...])[: n.deg]
        for m in range(n.ml):
            v.sww[t, m * n.deg : (m + 1) * n.deg, :] = block

    arrived("a1", v.r1.at[pl.ds(0, n.nb - 1)])
    spectrum = v.r1[...].reshape(total_rows, LANES)
    coeffs = jnp.dot(v.qa[...], spectrum, preferred_element_type=f32)
    v.coeffs[...] = coeffs
    real, imag = coeffs[:half], coeffs[half:]
    s0, s1 = v.sww[0], v.sww[1]
    filtered = jnp.concatenate([s0 * real - s1 * imag, s0 * imag + s1 * real], axis=0)
    synth = jnp.dot(v.pb[...], filtered.astype(bf16), preferred_element_type=f32)
    v.s2[...] = synth.astype(bf16).reshape(n.nb, piece, LANES)
    exchange("a2", "lat", me_b, n.nb, v.s2, v.r2)

    v.square[...] = jnp.zeros((LANES, LANES), f32)
    v.square[: n.ks, : n.cl] = v.dw[...]
    columns = jnp.transpose(v.square[...])
    for k in range(n.ks):
        v.wcol[k] = jnp.broadcast_to(columns[: n.cl, k : k + 1], (n.cl, n.lon))
    arrived("lo", v.halo.at[0])
    arrived("hi", v.halo.at[1])
    for r in range(HALO):
        v.fext[r] = v.halo[0, r].astype(f32)
        v.fext[HALO + n.rows + r] = v.halo[1, r].astype(f32)

    for r in range(n.rows):

        def tap(k, total, r=r):
            source = v.rows[k, first + r] - first + HALO
            source = jnp.minimum(jnp.maximum(source, 0), n.rows + 2 * HALO - 1)
            amount = lax.rem(n.lon - v.shift[k, first + r], n.lon)
            moved = pltpu.roll(v.fext[source], amount, 1)
            v.shifted[r * n.ks + k] = moved
            return total + (v.coef[k, first + r] * v.wcol[k]) * moved

        v.disco[r] = lax.fori_loop(0, n.ks, tap, jnp.zeros((n.cl, n.lon), f32))

    for t in range(2):
        mine = slice(t * half, (t + 1) * half)
        v.qb[:, mine] = jnp.transpose(v.qa[mine, :].astype(f32)).astype(bf16)
    v.wht[...] = jnp.transpose(v.wh[...].astype(f32)).astype(bf16)
    arrived("cot", v.cotall.at[pl.ds(0, n.ng - 1)])
    v.gact[...] = jnp.dot(
        v.wo[...], v.cotall[...].reshape(n.chans, LANES), preferred_element_type=f32
    )

    arrived("a2", v.r2.at[pl.ds(0, n.nb - 1)])
    for r, row in enumerate(from_pieces(v.inv, v.r2)):
        mixed = (row + v.disco[r]).astype(bf16)
        v.mixs[2 * r] = mixed[:, :LANES]
        v.mixs[2 * r + 1] = mixed[:, LANES:]
    exchange("mix", "chan", me_g, n.ng, v.mixs, v.mixall)

    arrived("mix", v.mixall.at[pl.ds(0, n.ng - 1)])
    mixed = v.mixall[...].reshape(n.chans, LANES).astype(f32)
    rscale = lax.rsqrt(jnp.sum(mixed * mixed, axis=0, keepdims=True) * (1.0 / n.chans) + norm_eps)
    normed32 = mixed * rscale
    normed = normed32.astype(bf16)
    v.n32[...] = normed32
    preact = jnp.dot(v.wht[...], normed, preferred_element_type=f32)
    cumulative = 0.5 * (1.0 + lax.erf(preact * inv_root_two))
    density = jnp.exp(-0.5 * preact * preact) * inv_root_tau
    activated = preact * cumulative
    grad_pre = (v.gact[...] * (cumulative + preact * density)).astype(bf16)
    v.gpre[...] = grad_pre
    grad_normed = jnp.dot(v.wh[...], grad_pre, preferred_element_type=f32)
    along = jnp.sum(grad_normed * normed32, axis=0, keepdims=True) * (1.0 / n.chans)
    grad_mixed = (rscale * (grad_normed - normed32 * along)).astype(bf16)
    v.gs[...] = grad_mixed.reshape(n.ng, n.cl, LANES)
    exchange("grd", "chan", me_g, n.ng, v.gs, v.gr)

    share = n.chans // n.nb
    for x in range(n.nx):
        for z in range(n.nz):
            at, to = (z * n.nx + x) * share, (x * n.nz + z) * share
            v.np32[to : to + share, :] = v.n32[at : at + share, :]
            v.ap32[2 * to : 2 * (to + share), :] = activated[2 * at : 2 * (at + share)]
    normed = v.np32[...].astype(bf16)
    activated = v.ap32[...].astype(bf16)
    adjoint = v.cotall[...].reshape(n.chans, LANES)
    cols, depth = n.chans // n.nx, n.hid // n.nx

    def r_a(k):
        for half in range(2):
            at = half * n.chans + k * LANES
            hidden = lax.dot_general(
                normed, v.gpre[at : at + LANES, :], NT, preferred_element_type=f32
            ).astype(bf16)
            for x in range(n.nx):
                rows = hidden[x * cols : (x + 1) * cols]
                v.was[0, k, x, half * cols : (half + 1) * cols, :] = rows
        output = lax.dot_general(
            activated, adjoint[k * LANES : (k + 1) * LANES], NT, preferred_element_type=f32
        )
        v.was[1, k] = output.astype(bf16).reshape(n.nx, depth, LANES)
        copy(f"ra{k}", v.was.at[1 - me_e, k], v.war.at[k], {"ens": 1 - me_e}).start()

    def r_b(k):
        arrived(f"ra{k}", v.war.at[k])
        v.wbs[k] = (v.was[me_e, k].astype(f32) + v.war[k].astype(f32)).astype(bf16)

        def send(t, carry):
            x = lax.rem(me_x + t, n.nx)
            copy(f"rb{k}", v.wbs.at[k, x], v.wbr.at[k, me_x], {"lat": me_z * n.nx + x}).start()
            return carry

        lax.fori_loop(1, n.nx, send, 0)
        v.wbr[k, me_x] = v.wbs[k, me_x]

    def r_c(k):
        arrived(f"rb{k}", v.wbr.at[k, pl.ds(0, n.nx - 1)])
        v.wsum[...] = jnp.sum(v.wbr[k].astype(f32), axis=0)

        @pl.when(me_e == 0)
        def _():
            for z in range(n.nz):
                for half in range(2):
                    at, to = half * cols + z * share, half * (n.slot // 2)
                    v.wslot[z, to : to + share, :] = v.wsum[at : at + share, :]

        @pl.when(me_e == 1)
        def _():
            for z in range(n.nz):
                v.wslot[z, : 2 * share, :] = v.wsum[2 * z * share : 2 * (z + 1) * share, :]

        v.wcs[k] = v.wslot[...].astype(bf16)

        def send(t, carry):
            z = lax.rem(me_z + t, n.nz)
            copy(f"rc{k}", v.wcs.at[k, z], v.wcr.at[k, me_z], {"lat": z * n.nx + me_x}).start()
            return carry

        lax.fori_loop(1, n.nz, send, 0)
        v.wcr[k, me_z] = v.wcs[k, me_z]

    def r_d(k):
        arrived(f"rc{k}", v.wcr.at[k, pl.ds(0, n.nz - 1)])
        v.wds[k] = jnp.sum(v.wcr[k].astype(f32), axis=0).astype(bf16)

        def send(t, carry):
            g = lax.rem(me_g + t, n.ng)
            copy(f"rd{k}", v.wds.at[k], v.wdr.at[k, me_g], {"chan": g}).start()
            return carry

        lax.fori_loop(1, n.ng, send, 0)
        v.wdr[k, me_g] = v.wds[k]

    def r_e(k):
        arrived(f"rd{k}", v.wdr.at[k, pl.ds(0, n.ng - 1)])
        v.wtot[me_e, k] = jnp.sum(v.wdr[k].astype(f32), axis=0)

    for k in range(n.kc):
        r_a(k)
    r_b(0)

    arrived("grd", v.gr.at[pl.ds(0, n.ng - 1)])
    for r in range(n.rows):
        v.gm[r] = jnp.concatenate([v.gr[2 * r], v.gr[2 * r + 1]], axis=1)
    to_pieces(v.inv, lambda r: v.gm[r], v.s5)
    exchange("a5", "lat", me_b, n.nb, v.s5, v.r5)
    copy("ghi", v.gm.at[top], v.ghalo.at[1], {"lat": below}).start()
    copy("glo", v.gm.at[bottom], v.ghalo.at[0], {"lat": above}).start()
    r_b(1)
    r_b(2)

    lane = lax.broadcasted_iota(jnp.int32, (n.cl, LANES), 1)

    def weight_tap(k, total):
        inner = jnp.zeros((n.cl, n.lon), f32)
        for r in range(n.rows):
            inner = inner + v.coef[k, first + r] * (
                v.shifted[r * n.ks + k] * v.gm[r].astype(f32)
            )
        return total + jnp.where(lane == k, jnp.sum(inner, axis=1, keepdims=True), 0.0)

    weight_grad = lax.fori_loop(0, n.ks, weight_tap, jnp.zeros((n.cl, LANES), f32))
    v.square[...] = jnp.zeros((LANES, LANES), f32)
    v.square[: n.cl, :] = weight_grad
    v.dgrad[...] = jnp.transpose(v.square[...])

    for r in range(n.rows):
        v.back[r] = jnp.zeros((n.cl, n.lon), f32)

    def spread(at, rows_of):
        values = rows_of.astype(f32)
        wanted = first - HALO + at
        held = jnp.minimum(jnp.maximum(wanted, 0), n.lat - 1)
        real_row = jnp.where(held == wanted, 1.0, 0.0).astype(f32)
        targets = [r for r in range(n.rows) if abs(at - HALO - r) <= HALO]

        def tap(k, totals):
            moved = pltpu.roll(values, lax.rem(n.lon + v.shift[k, held], n.lon), 1) * v.wcol[k]
            factor = v.coef[k, held] * real_row
            to = v.rows[k, held]
            return tuple(
                total + jnp.where(to == first + r, factor, 0.0) * moved
                for r, total in zip(targets, totals)
            )

        start = tuple(v.back[r] for r in targets)
        for r, total in zip(targets, lax.fori_loop(0, n.ks, tap, start)):
            v.back[r] = total

    for r in range(n.rows):
        if r == n.rows // 2:
            r_c(0)
        spread(HALO + r, v.gm[r])

    arrived("a5", v.r5.at[pl.ds(0, n.nb - 1)])
    grads = jnp.dot(v.pa[...], v.r5[...].reshape(total_rows, LANES), preferred_element_type=f32)
    g_real, g_imag = grads[:half], grads[half:]
    s0, s1 = v.sww[0], v.sww[1]
    g_coeffs = jnp.concatenate([s0 * g_real + s1 * g_imag, s0 * g_imag - s1 * g_real], axis=0)
    back_spec = jnp.dot(v.qb[...], g_coeffs.astype(bf16), preferred_element_type=f32)
    v.s6[...] = back_spec.astype(bf16).reshape(n.nb, piece, LANES)
    exchange("a6", "lat", me_b, n.nb, v.s6, v.r6)

    real, imag = v.coeffs[:half, :], v.coeffs[half:, :]
    terms = (g_real * real + g_imag * imag, g_imag * real - g_real * imag)
    disco_part = pltpu.roll(v.dgrad[: n.frows, :], 64, 1)
    low_lanes = lax.broadcasted_iota(jnp.int32, (n.frows, LANES), 1) < 64
    for t in range(2):
        part = terms[t][: n.deg]
        for m in range(1, n.ml):
            part = part + terms[t][m * n.deg : (m + 1) * n.deg]
        for x in range(n.nx):
            rows = part[x * n.frows : (x + 1) * n.frows]
            v.fas[t * n.nx + x] = jnp.where(low_lanes, rows, disco_part).astype(bf16)
    place = me_e * n.nx + me_x

    def near(t):
        p = lax.rem(place + t, 2 * n.nx)
        return p, {"ens": lax.div(p, n.nx), "lat": me_z * n.nx + lax.rem(p, n.nx)}

    def send_fa(t, carry):
        p, to = near(t)
        copy("fa", v.fas.at[p], v.far.at[place], to).start()
        return carry

    lax.fori_loop(1, 2 * n.nx, send_fa, 0)
    v.far[place] = v.fas[place]
    r_c(1)

    arrived("glo", v.ghalo.at[0])
    arrived("ghi", v.ghalo.at[1])
    spread(0, v.ghalo[0, 0])
    spread(1, v.ghalo[0, 1])

    arrived("fa", v.far.at[pl.ds(0, 2 * n.nx - 1)])
    v.fbs[...] = jnp.sum(v.far[...].astype(f32), axis=0).astype(bf16)

    def send_fb(t, carry):
        z = lax.rem(me_z + t, n.nz)
        copy("fb", v.fbs, v.fbr.at[me_z], {"lat": z * n.nx + me_x}).start()
        return carry

    lax.fori_loop(1, n.nz, send_fb, 0)
    v.fbr[me_z] = v.fbs[...]
    r_c(2)
    r_d(0)

    spread(HALO + n.rows, v.ghalo[1, 0])
    spread(HALO + n.rows + 1, v.ghalo[1, 1])
    r_d(1)
    r_d(2)

    arrived("a6", v.r6.at[pl.ds(0, n.nb - 1)])
    for r, row in enumerate(from_pieces(v.fwd, v.r6)):
        base = jnp.concatenate([v.cot8[2 * r], v.cot8[2 * r + 1]], axis=1).astype(f32)
        v.wide[:, r, :] = base + row + v.back[r]
    v.gfield[...] = v.wide[...].astype(bf16)

    arrived("fb", v.fbr.at[pl.ds(0, n.nz - 1)])
    ftot = jnp.sum(v.fbr[...].astype(f32), axis=0)
    v.fcr[place] = ftot

    def send_fc(t, carry):
        p, to = near(t)
        copy("fc", v.fcr.at[place], v.fcr.at[place], to).start()
        return carry

    lax.fori_loop(1, 2 * n.nx, send_fc, 0)
    v.gdw[...] = pltpu.roll(ftot, 64, 1)[: n.ks, : n.cl] * n.scale

    for k in range(n.kc):
        r_e(k)
    copy("re", v.wtot.at[me_e], v.wtot.at[me_e], {"ens": 1 - me_e}).start()

    arrived("fc", v.fcr.at[pl.ds(0, 2 * n.nx - 1)])
    flipped = jnp.transpose(v.fcr[...].reshape(2 * n.deg, LANES))
    for t in range(2):
        v.gsw[t] = flipped[: n.cl, t * n.deg : (t + 1) * n.deg]

    arrived("re", v.wtot.at[0])
    for k in range(n.kc):
        lanes = slice(k * LANES, (k + 1) * LANES)
        upper = slice(n.chans + k * LANES, n.chans + (k + 1) * LANES)
        low = n.slot // 2
        v.gh[:, lanes] = v.wtot[0, k, :share, :] * n.scale
        v.gh[:, upper] = v.wtot[0, k, low : low + share, :] * n.scale
        v.go[:, lanes] = v.wtot[1, k, : 2 * share, :] * n.scale

    for phase, ref in (("a1", v.s1), ("a2", v.s2), ("a5", v.s5), ("a6", v.s6)):
        left(phase, ref.at[pl.ds(0, n.nb - 1)])
    for phase, ref in (("cot", v.cot8), ("mix", v.mixs), ("grd", v.gs)):
        left(phase, ref.at[pl.ds(0, n.ng - 1)])
    left("hi", v.halo.at[1])
    left("lo", v.halo.at[0])
    left("ghi", v.ghalo.at[1])
    left("glo", v.ghalo.at[0])
    for k in range(n.kc):
        left(f"ra{k}", v.war.at[k])
        left(f"rb{k}", v.wbs.at[k, pl.ds(0, n.nx - 1)])
        left(f"rc{k}", v.wcs.at[k, pl.ds(0, n.nz - 1)])
        left(f"rd{k}", v.wdr.at[k, pl.ds(0, n.ng - 1)])
    left("re", v.wtot.at[0])
    left("fa", v.fas.at[pl.ds(0, 2 * n.nx - 1)])
    left("fb", v.fbr.at[pl.ds(0, n.nz - 1)])
    left("fc", v.fcr.at[pl.ds(0, 2 * n.nx - 1)])


class Sizes:
    pass


def copies(*refs):
    count = len(refs) // 2
    sems = refs[-1]
    moves = [
        pltpu.make_async_copy(refs[i], refs[count + i], sems.at[i]) for i in range(count)
    ]
    for move in moves:
        move.start()
    for move in moves:
        move.wait()


def shards(
    nx,
    field,
    cotangent,
    spec_weight,
    disco_coef,
    disco_weight,
    disco_rows,
    disco_shift,
    w_hidden,
    w_output,
):
    n = Sizes()
    _, n.cl, n.rows, n.lon = field.shape
    n.ne, n.nb, n.ng = (lax.axis_size(a) for a in ("ens", "lat", "chan"))
    n.nx = nx
    n.nz = n.nb // nx
    n.lat = n.rows * n.nb
    n.modes = n.lat // 2
    n.ml = n.modes // n.nb
    n.qn = 2 * n.ml
    n.deg = spec_weight.shape[1]
    n.ks = disco_coef.shape[1]
    n.chans, n.hid = w_hidden.shape
    n.frows = n.deg // n.nx
    n.kc = n.chans // LANES
    n.slot = 2 * (-(-(n.chans // n.nb) // 16) * 16)
    n.scale = 1.0 / math.sqrt(n.ne * n.lat * n.lon)
    plain, weighted, forward, inverse = constant_tables(n.lat, n.lon, n.modes, n.deg, n.nb)
    scratches = scratch(n)
    vmem = pl.BlockSpec(memory_space=pltpu.VMEM)
    smem = pl.BlockSpec(memory_space=pltpu.SMEM)
    hbm = pl.BlockSpec(memory_space=pl.ANY)
    share = n.chans // n.nb
    shapes = (
        jax.ShapeDtypeStruct((n.cl, n.rows, n.lon), bf16),
        jax.ShapeDtypeStruct((2, n.cl, n.deg), f32),
        jax.ShapeDtypeStruct((n.ks, n.cl), f32),
        jax.ShapeDtypeStruct((share, n.hid), f32),
        jax.ShapeDtypeStruct((2 * share, n.chans), f32),
    )
    results = pl.pallas_call(
        functools.partial(kernel, n, ARGS + tuple(scratches)),
        out_shape=shapes,
        in_specs=[vmem] * 8 + [smem] * 3 + [hbm] * 2,
        out_specs=(vmem,) * 5,
        scratch_shapes=list(scratches.values()),
        compiler_params=pltpu.CompilerParams(
            collective_id=0, has_side_effects=True, vmem_limit_bytes=56 * 1024 * 1024
        ),
    )(
        field[0],
        cotangent[0],
        jnp.transpose(spec_weight, (0, 2, 1)),
        disco_weight,
        w_hidden,
        w_output,
        jnp.asarray(forward),
        jnp.asarray(inverse),
        jnp.transpose(disco_coef),
        jnp.transpose(disco_rows),
        jnp.transpose(disco_shift),
        jnp.asarray(plain),
        jnp.asarray(weighted),
    )
    grad_field, grad_spec, grad_disco, grad_hidden, grad_output = pl.pallas_call(
        copies,
        out_shape=shapes,
        in_specs=[hbm] * len(shapes),
        out_specs=(hbm,) * len(shapes),
        scratch_shapes=[pltpu.SemaphoreType.DMA((len(shapes),))],
    )(*results)
    return (
        grad_field[None],
        jnp.transpose(grad_spec, (0, 2, 1)),
        grad_disco,
        grad_hidden,
        grad_output,
    )


def solution(mesh, nx=4):
    in_specs = (
        P("ens", "chan", "lat", None),
        P("ens", "chan", "lat", None),
        P(None, None, "chan"),
        P(),
        P(None, "chan"),
        P(),
        P(),
        P(),
        P(),
    )
    out_specs = (
        P("ens", "chan", "lat", None),
        P(None, None, "chan"),
        P(None, "chan"),
        P("lat", None),
        P("lat", None),
    )
    return jax.shard_map(
        functools.partial(shards, nx),
        mesh=mesh,
        in_specs=in_specs,
        out_specs=out_specs,
        check_vma=False,
    )
```

```python
import functools
import math

import jax
import jax.numpy as jnp
import ml_dtypes
import numpy as np
from jax import lax
from jax.experimental import pallas as pl
from jax.experimental.pallas import tpu as pltpu
from jax.sharding import PartitionSpec as P

MESH = pl.DeviceIdType.MESH
HALO = 2
LANES = 128
norm_eps = 1e-06
inv_root_two = 0.7071067811865476
inv_root_tau = 0.3989422804014327
f32 = jnp.float32
bf16 = jnp.bfloat16
NT = (((1,), (1,)), ((), ()))


def legendre_table(lat_count, order_count, degree_count):
    theta = math.pi * (np.arange(lat_count) + 0.5) / lat_count
    cosine, sine = np.cos(theta), np.sin(theta)
    table = np.zeros((order_count, degree_count, lat_count))
    for m in range(order_count):
        start = 0.5 * (
            math.log((2 * m + 1) / (4 * math.pi))
            + math.lgamma(m + 0.5)
            - math.lgamma(m + 1)
            - math.lgamma(0.5)
        )
        if m < degree_count:
            table[m, m] = np.exp(start + m * np.log(sine))
        for l in range(m + 1, degree_count):
            a = math.sqrt((4 * l * l - 1) / (l * l - m * m))
            b = math.sqrt(((l - 1) ** 2 - m * m) / (4 * (l - 1) ** 2 - 1))
            before = table[m, l - 2] if l >= 2 else 0.0
            table[m, l] = a * (cosine * table[m, l - 1] - b * before)
    return table


def constant_tables(lat_count, lon_count, mode_count, degree_count, bands):
    legendre = legendre_table(lat_count, mode_count, degree_count)
    sine = np.sin(math.pi * (np.arange(lat_count) + 0.5) / lat_count)
    quadrature = (2 * math.pi / lon_count) * (math.pi / lat_count) * sine
    here = mode_count // bands
    shape = (bands, here * degree_count, lat_count)
    plain = legendre.reshape(shape).astype(np.float32).astype(ml_dtypes.bfloat16)
    weighted = (legendre * quadrature).reshape(shape).astype(np.float32).astype(ml_dtypes.bfloat16)
    modes = np.arange(mode_count)
    phase = 2 * math.pi * ((modes[:, None] * np.arange(lon_count)[None, :]) % lon_count) / lon_count
    scale = np.where(modes == 0, 1.0, 2.0)[:, None]
    cos_rows = np.cos(phase).reshape(bands, 1, here, lon_count)
    sin_rows = -np.sin(phase).reshape(bands, 1, here, lon_count)
    forward = np.concatenate([cos_rows, sin_rows], axis=1).reshape(2 * mode_count, lon_count)
    doubled = np.repeat(scale.reshape(bands, 1, here, 1), 2, axis=1).reshape(2 * mode_count, 1)
    cast = lambda v: v.astype(np.float32).astype(ml_dtypes.bfloat16)
    return plain, weighted, cast(forward), cast(forward * doubled)


class Names:
    def __init__(self, names, refs):
        for name, ref in zip(names, refs, strict=True):
            setattr(self, name, ref)


ARGS = (
    "field", "cot", "sw", "dw", "wh", "wo", "fwd", "inv", "coef", "rows", "shift", "p_hbm",
    "q_hbm", "gfield", "gsw", "gdw", "gh", "go",
)
DMAS = (
    "a1", "a2", "cot", "mix", "grd", "a5", "a6", "lo", "hi", "glo", "ghi", "re", "fa", "fb", "fc",
    "ra0", "ra1", "ra2", "rb0", "rb1", "rb2", "rc0", "rc1", "rc2", "rd0", "rd1", "rd2",
)
S = {name: i for i, name in enumerate(DMAS)}


def scratch(n):
    piece = n.qn * n.rows
    return dict(
        pt=pltpu.VMEM((n.ml * n.deg, n.lat), bf16),
        qt=pltpu.VMEM((n.ml * n.deg, n.lat), bf16),
        qa=pltpu.VMEM((n.qn * n.deg, n.nb * piece), bf16),
        pa=pltpu.VMEM((n.qn * n.deg, n.nb * piece), bf16),
        qb=pltpu.VMEM((n.nb * piece, n.qn * n.deg), bf16),
        pb=pltpu.VMEM((n.nb * piece, n.qn * n.deg), bf16),
        wht=pltpu.VMEM((n.hid, n.chans), bf16),
        spread_rows=pltpu.VMEM((n.nb * piece, LANES), f32),
        s1=pltpu.VMEM((n.nb, piece, LANES), bf16),
        r1=pltpu.VMEM((n.nb, piece, LANES), bf16),
        s2=pltpu.VMEM((n.nb, piece, LANES), bf16),
        r2=pltpu.VMEM((n.nb, piece, LANES), bf16),
        s5=pltpu.VMEM((n.nb, piece, LANES), bf16),
        r5=pltpu.VMEM((n.nb, piece, LANES), bf16),
        s6=pltpu.VMEM((n.nb, piece, LANES), bf16),
        r6=pltpu.VMEM((n.nb, piece, LANES), bf16),
        coeffs=pltpu.VMEM((n.qn * n.deg, LANES), f32),
        sww=pltpu.VMEM((2, n.ml * n.deg, LANES), f32),
        halo=pltpu.VMEM((2, HALO, n.cl, n.lon), bf16),
        ghalo=pltpu.VMEM((2, HALO, n.cl, n.lon), bf16),
        fext=pltpu.VMEM((n.rows + 2 * HALO, n.cl, n.lon), f32),
        gm=pltpu.VMEM((n.rows, n.cl, n.lon), bf16),
        shifted=pltpu.VMEM((n.rows * n.ks, n.cl, n.lon), f32),
        square=pltpu.VMEM((LANES, LANES), f32),
        wcol=pltpu.VMEM((n.ks, n.cl, n.lon), f32),
        disco=pltpu.VMEM((n.rows, n.cl, n.lon), f32),
        back=pltpu.VMEM((n.rows, n.cl, n.lon), f32),
        dgrad=pltpu.VMEM((LANES, LANES), f32),
        cotall=pltpu.VMEM((n.ng, n.cl, LANES), bf16),
        mixs=pltpu.VMEM((n.ng, n.cl, LANES), bf16),
        mixall=pltpu.VMEM((n.ng, n.cl, LANES), bf16),
        gact=pltpu.VMEM((n.hid, LANES), f32),
        gpre=pltpu.VMEM((n.hid, LANES), bf16),
        gs=pltpu.VMEM((n.ng, n.cl, LANES), bf16),
        gr=pltpu.VMEM((n.ng, n.cl, LANES), bf16),
        wide=pltpu.VMEM((n.cl, n.rows, n.lon), f32),
        fld=pltpu.VMEM((n.rows, n.cl, n.lon), bf16),
        cot8=pltpu.VMEM((n.ng, n.cl, LANES), bf16),
        n32=pltpu.VMEM((n.chans, LANES), f32),
        np32=pltpu.VMEM((n.chans, LANES), f32),
        ap32=pltpu.VMEM((n.hid, LANES), f32),
        was=pltpu.VMEM((2, n.kc, n.nx, n.hid // n.nx, LANES), bf16),
        war=pltpu.VMEM((n.kc, n.nx, n.hid // n.nx, LANES), bf16),
        wbs=pltpu.VMEM((n.kc, n.nx, n.hid // n.nx, LANES), bf16),
        wbr=pltpu.VMEM((n.kc, n.nx, n.hid // n.nx, LANES), bf16),
        wsum=pltpu.VMEM((n.hid // n.nx, LANES), f32),
        wslot=pltpu.VMEM((n.nz, n.slot, LANES), f32),
        wcs=pltpu.VMEM((n.kc, n.nz, n.slot, LANES), bf16),
        wcr=pltpu.VMEM((n.kc, n.nz, n.slot, LANES), bf16),
        wds=pltpu.VMEM((n.kc, n.slot, LANES), bf16),
        wdr=pltpu.VMEM((n.kc, n.ng, n.slot, LANES), bf16),
        wtot=pltpu.VMEM((2, n.kc, n.slot, LANES), f32),
        fas=pltpu.VMEM((2 * n.nx, n.frows, LANES), bf16),
        far=pltpu.VMEM((2 * n.nx, n.frows, LANES), bf16),
        fbs=pltpu.VMEM((n.frows, LANES), bf16),
        fbr=pltpu.VMEM((n.nz, n.frows, LANES), bf16),
        fcr=pltpu.VMEM((2 * n.nx, n.frows, LANES), f32),
        load_sem=pltpu.SemaphoreType.DMA((2,)),
        send=pltpu.SemaphoreType.DMA((len(DMAS),)),
        recv=pltpu.SemaphoreType.DMA((len(DMAS),)),
    )


def kernel(n, names, *refs):
    v = Names(list(names), refs)
    me_e, me_b, me_g = (lax.axis_index(a) for a in ("ens", "lat", "chan"))
    me_z, me_x = lax.div(me_b, n.nx), lax.rem(me_b, n.nx)
    first = me_b * n.rows
    piece = n.qn * n.rows
    total_rows = n.nb * piece

    def copy(phase, src, dst, device):
        return pltpu.make_async_remote_copy(
            src_ref=src,
            dst_ref=dst,
            send_sem=v.send.at[S[phase]],
            recv_sem=v.recv.at[S[phase]],
            device_id=device,
            device_id_type=MESH,
        )

    def arrived(phase, ref):
        pltpu.make_async_copy(ref, ref, v.recv.at[S[phase]]).wait()

    def left(phase, ref):
        pltpu.make_async_copy(ref, ref, v.send.at[S[phase]]).wait()

    def lat_peer(k):
        return lax.rem(me_b + k, n.nb)

    def farthest_first(t, count):
        return count // 2 + jnp.where(lax.rem(t, 2) == 0, -lax.div(t, 2), lax.div(t + 1, 2))

    def lat_at(t):
        u = lax.div(t, n.nx)
        far = n.nz // 2
        dz = jnp.where(lax.rem(u, 2) == 0, far - lax.div(u, 2), far + lax.div(u + 1, 2))
        dx = lax.rem(n.nx // 2 + n.nx - lax.rem(t, n.nx), n.nx)
        dx = jnp.where(u == n.nz - 1, n.nx // 2 + lax.rem(t, n.nx) - 1, dx)
        return lax.rem(me_z + n.nz + dz, n.nz) * n.nx + lax.rem(me_x + n.nx + dx, n.nx)

    def exchange(phase, axis, me, count, src, dst, whole=False):
        def step(k, carry):
            d = lax.rem(me + farthest_first(k, count), count)
            copy(phase, src if whole else src.at[d], dst.at[me], {axis: d}).start()
            return carry

        def to_lat(t, carry):
            d = lat_at(t)
            copy(phase, src.at[d], dst.at[me], {axis: d}).start()
            return carry

        if axis == "lat":
            lax.fori_loop(0, count - 1, to_lat, 0, unroll=True)
        else:
            lax.fori_loop(0, count - 1, step, 0)
        dst[me] = src[...] if whole else src[me]

    barrier = pltpu.get_barrier_semaphore()

    def greet(device):
        pl.semaphore_signal(barrier, inc=1, device_id=device, device_id_type=MESH)

    def greet_lat(k, carry):
        greet({"lat": lat_at(k)})
        return carry

    def greet_chan(k, carry):
        greet({"chan": lax.rem(me_g + k, n.ng)})
        return carry

    def greet_ens(k, carry):
        greet({"ens": 1 - me_e, "lat": me_z * n.nx + k})
        return carry

    lax.fori_loop(0, n.nb - 1, greet_lat, 0)
    lax.fori_loop(1, n.ng, greet_chan, 0)
    lax.fori_loop(0, n.nx, greet_ens, 0)

    load_p = pltpu.make_async_copy(v.p_hbm.at[me_b], v.pt, v.load_sem.at[0])
    load_q = pltpu.make_async_copy(v.q_hbm.at[me_b], v.qt, v.load_sem.at[1])
    load_p.start()
    load_q.start()

    def to_pieces(table, row_of, out):
        for r in range(n.rows):
            part = lax.dot_general(table[...], row_of(r), NT, preferred_element_type=f32)
            v.spread_rows[pl.ds(r, 2 * n.modes, stride=n.rows), :] = jnp.concatenate(
                [part, jnp.zeros((2 * n.modes, LANES - n.cl), f32)], axis=1
            )
        out[...] = v.spread_rows[...].astype(bf16).reshape(n.nb, piece, LANES)

    def from_pieces(table, pieces):
        v.spread_rows[...] = pieces[...].reshape(total_rows, LANES).astype(f32)
        rows = []
        for r in range(n.rows):
            part = v.spread_rows[pl.ds(r, 2 * n.modes, stride=n.rows), :]
            flipped = jnp.transpose(part).astype(bf16)[: n.cl]
            rows.append(jnp.dot(flipped, table[...], preferred_element_type=f32))
        return rows

    v.wide[...] = v.field[...].astype(f32)
    for r in range(n.rows):
        row = v.wide[:, r, :]
        v.fext[HALO + r] = row
        v.fld[r] = row.astype(bf16)
    to_pieces(v.fwd, lambda r: v.fld[r], v.s1)
    v.wide[...] = v.cot[...].astype(f32)
    for r in range(n.rows):
        row = v.wide[:, r, :].astype(bf16)
        v.cot8[2 * r] = row[:, :LANES]
        v.cot8[2 * r + 1] = row[:, LANES:]
    pl.semaphore_wait(barrier, n.nb - 1 + n.ng - 1 + n.nx)

    exchange("a1", "lat", me_b, n.nb, v.s1, v.r1)
    below, above = lat_peer(n.nb - 1), lat_peer(1)
    top, bottom = pl.ds(0, HALO), pl.ds(n.rows - HALO, HALO)
    copy("hi", v.fld.at[top], v.halo.at[1], {"lat": below}).start()
    copy("lo", v.fld.at[bottom], v.halo.at[0], {"lat": above}).start()
    exchange("cot", "chan", me_g, n.ng, v.cot8, v.cotall)

    load_p.wait()
    load_q.wait()

    half = n.ml * n.deg
    wide = (n.lat, total_rows)
    column = lax.broadcasted_iota(jnp.int32, wide, 1)
    row_id = lax.broadcasted_iota(jnp.int32, wide, 0)
    lat_of = lax.div(column, piece) * n.rows + lax.rem(column, n.rows)
    expand = jnp.where(lat_of == row_id, 1.0, 0.0).astype(bf16)
    q_of = lax.div(lax.rem(lax.broadcasted_iota(jnp.int32, (half, total_rows), 1), piece), n.rows)
    ml_of = lax.div(lax.broadcasted_iota(jnp.int32, (half, total_rows), 0), n.deg)

    def expanded(table, out):
        both = jnp.dot(table[...], expand, preferred_element_type=f32)
        for t in range(2):
            keep = q_of == ml_of + t * n.ml
            out[t * half : (t + 1) * half, :] = jnp.where(keep, both, 0.0).astype(bf16)

    expanded(v.qt, v.qa)
    expanded(v.pt, v.pa)
    for t in range(2):
        mine = slice(t * half, (t + 1) * half)
        v.pb[:, mine] = jnp.transpose(v.pa[mine, :].astype(f32)).astype(bf16)
    v.square[...] = jnp.zeros((LANES, LANES), f32)
    for t in range(2):
        v.square[: n.cl, : n.deg] = v.sw[t]
        block = jnp.transpose(v.square[...])[: n.deg]
        for m in range(n.ml):
            v.sww[t, m * n.deg : (m + 1) * n.deg, :] = block

    arrived("a1", v.r1.at[pl.ds(0, n.nb - 1)])
    spectrum = v.r1[...].reshape(total_rows, LANES)
    coeffs = jnp.dot(v.qa[...], spectrum, preferred_element_type=f32)
    v.coeffs[...] = coeffs
    real, imag = coeffs[:half], coeffs[half:]
    s0, s1 = v.sww[0], v.sww[1]
    filtered = jnp.concatenate([s0 * real - s1 * imag, s0 * imag + s1 * real], axis=0)
    synth = jnp.dot(v.pb[...], filtered.astype(bf16), preferred_element_type=f32)
    v.s2[...] = synth.astype(bf16).reshape(n.nb, piece, LANES)
    exchange("a2", "lat", me_b, n.nb, v.s2, v.r2)

    v.square[...] = jnp.zeros((LANES, LANES), f32)
    v.square[: n.ks, : n.cl] = v.dw[...]
    columns = jnp.transpose(v.square[...])
    for k in range(n.ks):
        v.wcol[k] = jnp.broadcast_to(columns[: n.cl, k : k + 1], (n.cl, n.lon))
    arrived("lo", v.halo.at[0])
    arrived("hi", v.halo.at[1])
    for r in range(HALO):
        v.fext[r] = v.halo[0, r].astype(f32)
        v.fext[HALO + n.rows + r] = v.halo[1, r].astype(f32)

    for r in range(n.rows):

        def tap(k, total, r=r):
            source = v.rows[k, first + r] - first + HALO
            source = jnp.minimum(jnp.maximum(source, 0), n.rows + 2 * HALO - 1)
            amount = lax.rem(n.lon - v.shift[k, first + r], n.lon)
            moved = pltpu.roll(v.fext[source], amount, 1)
            v.shifted[r * n.ks + k] = moved
            return total + (v.coef[k, first + r] * v.wcol[k]) * moved

        v.disco[r] = lax.fori_loop(0, n.ks, tap, jnp.zeros((n.cl, n.lon), f32), unroll=True)

    for t in range(2):
        mine = slice(t * half, (t + 1) * half)
        v.qb[:, mine] = jnp.transpose(v.qa[mine, :].astype(f32)).astype(bf16)
    v.wht[...] = jnp.transpose(v.wh[...].astype(f32)).astype(bf16)
    arrived("cot", v.cotall.at[pl.ds(0, n.ng - 1)])
    v.gact[...] = jnp.dot(
        v.wo[...], v.cotall[...].reshape(n.chans, LANES), preferred_element_type=f32
    )

    arrived("a2", v.r2.at[pl.ds(0, n.nb - 1)])
    for r, row in enumerate(from_pieces(v.inv, v.r2)):
        mixed = (row + v.disco[r]).astype(bf16)
        v.mixs[2 * r] = mixed[:, :LANES]
        v.mixs[2 * r + 1] = mixed[:, LANES:]
    exchange("mix", "chan", me_g, n.ng, v.mixs, v.mixall)

    arrived("mix", v.mixall.at[pl.ds(0, n.ng - 1)])
    mixed = v.mixall[...].reshape(n.chans, LANES).astype(f32)
    rscale = lax.rsqrt(jnp.sum(mixed * mixed, axis=0, keepdims=True) * (1.0 / n.chans) + norm_eps)
    normed32 = mixed * rscale
    normed = normed32.astype(bf16)
    v.n32[...] = normed32
    preact = jnp.dot(v.wht[...], normed, preferred_element_type=f32)
    cumulative = 0.5 * (1.0 + lax.erf(preact * inv_root_two))
    density = jnp.exp(-0.5 * preact * preact) * inv_root_tau
    activated = preact * cumulative
    grad_pre = (v.gact[...] * (cumulative + preact * density)).astype(bf16)
    v.gpre[...] = grad_pre
    grad_normed = jnp.dot(v.wh[...], grad_pre, preferred_element_type=f32)
    along = jnp.sum(grad_normed * normed32, axis=0, keepdims=True) * (1.0 / n.chans)
    grad_mixed = (rscale * (grad_normed - normed32 * along)).astype(bf16)
    v.gs[...] = grad_mixed.reshape(n.ng, n.cl, LANES)
    exchange("grd", "chan", me_g, n.ng, v.gs, v.gr)

    share = n.chans // n.nb
    for x in range(n.nx):
        for z in range(n.nz):
            at, to = (z * n.nx + x) * share, (x * n.nz + z) * share
            v.np32[to : to + share, :] = v.n32[at : at + share, :]
            v.ap32[2 * to : 2 * (to + share), :] = activated[2 * at : 2 * (at + share)]
    normed = v.np32[...].astype(bf16)
    activated = v.ap32[...].astype(bf16)
    adjoint = v.cotall[...].reshape(n.chans, LANES)
    cols, depth = n.chans // n.nx, n.hid // n.nx

    def r_a(k):
        for half in range(2):
            at = half * n.chans + k * LANES
            hidden = lax.dot_general(
                normed, v.gpre[at : at + LANES, :], NT, preferred_element_type=f32
            ).astype(bf16)
            for x in range(n.nx):
                rows = hidden[x * cols : (x + 1) * cols]
                v.was[0, k, x, half * cols : (half + 1) * cols, :] = rows
        output = lax.dot_general(
            activated, adjoint[k * LANES : (k + 1) * LANES], NT, preferred_element_type=f32
        )
        v.was[1, k] = output.astype(bf16).reshape(n.nx, depth, LANES)
        copy(f"ra{k}", v.was.at[1 - me_e, k], v.war.at[k], {"ens": 1 - me_e}).start()

    def r_b(k):
        arrived(f"ra{k}", v.war.at[k])
        v.wbs[k] = (v.was[me_e, k].astype(f32) + v.war[k].astype(f32)).astype(bf16)

        def send(t, carry):
            x = lax.rem(me_x + t, n.nx)
            copy(f"rb{k}", v.wbs.at[k, x], v.wbr.at[k, me_x], {"lat": me_z * n.nx + x}).start()
            return carry

        lax.fori_loop(1, n.nx, send, 0)
        v.wbr[k, me_x] = v.wbs[k, me_x]

    def r_c(k):
        arrived(f"rb{k}", v.wbr.at[k, pl.ds(0, n.nx - 1)])
        v.wsum[...] = jnp.sum(v.wbr[k].astype(f32), axis=0)

        @pl.when(me_e == 0)
        def _():
            for z in range(n.nz):
                for half in range(2):
                    at, to = half * cols + z * share, half * (n.slot // 2)
                    v.wslot[z, to : to + share, :] = v.wsum[at : at + share, :]

        @pl.when(me_e == 1)
        def _():
            for z in range(n.nz):
                v.wslot[z, : 2 * share, :] = v.wsum[2 * z * share : 2 * (z + 1) * share, :]

        v.wcs[k] = v.wslot[...].astype(bf16)

        def send(t, carry):
            z = lax.rem(me_z + t, n.nz)
            copy(f"rc{k}", v.wcs.at[k, z], v.wcr.at[k, me_z], {"lat": z * n.nx + me_x}).start()
            return carry

        lax.fori_loop(1, n.nz, send, 0)
        v.wcr[k, me_z] = v.wcs[k, me_z]

    def r_d(k):
        arrived(f"rc{k}", v.wcr.at[k, pl.ds(0, n.nz - 1)])
        v.wds[k] = jnp.sum(v.wcr[k].astype(f32), axis=0).astype(bf16)

        def send(t, carry):
            g = lax.rem(me_g + t, n.ng)
            copy(f"rd{k}", v.wds.at[k], v.wdr.at[k, me_g], {"chan": g}).start()
            return carry

        lax.fori_loop(1, n.ng, send, 0)
        v.wdr[k, me_g] = v.wds[k]

    def r_e(k):
        arrived(f"rd{k}", v.wdr.at[k, pl.ds(0, n.ng - 1)])
        v.wtot[me_e, k] = jnp.sum(v.wdr[k].astype(f32), axis=0)

    for k in range(n.kc):
        r_a(k)
    r_b(0)

    arrived("grd", v.gr.at[pl.ds(0, n.ng - 1)])
    for r in range(n.rows):
        v.gm[r] = jnp.concatenate([v.gr[2 * r], v.gr[2 * r + 1]], axis=1)
    to_pieces(v.inv, lambda r: v.gm[r], v.s5)
    exchange("a5", "lat", me_b, n.nb, v.s5, v.r5)
    copy("ghi", v.gm.at[top], v.ghalo.at[1], {"lat": below}).start()
    copy("glo", v.gm.at[bottom], v.ghalo.at[0], {"lat": above}).start()
    r_b(1)
    r_b(2)

    lane = lax.broadcasted_iota(jnp.int32, (n.cl, LANES), 1)

    def weight_tap(k, total):
        inner = jnp.zeros((n.cl, n.lon), f32)
        for r in range(n.rows):
            inner = inner + v.coef[k, first + r] * (
                v.shifted[r * n.ks + k] * v.gm[r].astype(f32)
            )
        return total + jnp.where(lane == k, jnp.sum(inner, axis=1, keepdims=True), 0.0)

    weight_grad = lax.fori_loop(
        0, n.ks, weight_tap, jnp.zeros((n.cl, LANES), f32), unroll=True
    )
    v.square[...] = jnp.zeros((LANES, LANES), f32)
    v.square[: n.cl, :] = weight_grad
    v.dgrad[...] = jnp.transpose(v.square[...])

    for r in range(n.rows):
        v.back[r] = jnp.zeros((n.cl, n.lon), f32)

    def spread(at, rows_of):
        values = rows_of.astype(f32)
        wanted = first - HALO + at
        held = jnp.minimum(jnp.maximum(wanted, 0), n.lat - 1)
        real_row = jnp.where(held == wanted, 1.0, 0.0).astype(f32)
        targets = [r for r in range(n.rows) if abs(at - HALO - r) <= HALO]

        def tap(k, totals):
            moved = pltpu.roll(values, lax.rem(n.lon + v.shift[k, held], n.lon), 1) * v.wcol[k]
            factor = v.coef[k, held] * real_row
            to = v.rows[k, held]
            return tuple(
                total + jnp.where(to == first + r, factor, 0.0) * moved
                for r, total in zip(targets, totals)
            )

        start = tuple(v.back[r] for r in targets)
        for r, total in zip(targets, lax.fori_loop(0, n.ks, tap, start, unroll=True)):
            v.back[r] = total

    for r in range(n.rows):
        if r == n.rows // 2:
            r_c(0)
        spread(HALO + r, v.gm[r])

    arrived("a5", v.r5.at[pl.ds(0, n.nb - 1)])
    grads = jnp.dot(v.pa[...], v.r5[...].reshape(total_rows, LANES), preferred_element_type=f32)
    g_real, g_imag = grads[:half], grads[half:]
    s0, s1 = v.sww[0], v.sww[1]
    g_coeffs = jnp.concatenate([s0 * g_real + s1 * g_imag, s0 * g_imag - s1 * g_real], axis=0)
    real, imag = v.coeffs[:half, :], v.coeffs[half:, :]
    terms = (g_real * real + g_imag * imag, g_imag * real - g_real * imag)
    disco_part = pltpu.roll(v.dgrad[: n.frows, :], 64, 1)
    low_lanes = lax.broadcasted_iota(jnp.int32, (n.frows, LANES), 1) < 64
    for t in range(2):
        part = terms[t][: n.deg]
        for m in range(1, n.ml):
            part = part + terms[t][m * n.deg : (m + 1) * n.deg]
        for x in range(n.nx):
            rows = part[x * n.frows : (x + 1) * n.frows]
            v.fas[t * n.nx + x] = jnp.where(low_lanes, rows, disco_part).astype(bf16)
    place = me_e * n.nx + me_x

    def near(t):
        p = lax.rem(place + t, 2 * n.nx)
        return p, {"ens": lax.div(p, n.nx), "lat": me_z * n.nx + lax.rem(p, n.nx)}

    def send_fa(t, carry):
        p, to = near(t)
        copy("fa", v.fas.at[p], v.far.at[place], to).start()
        return carry

    lax.fori_loop(1, 2 * n.nx, send_fa, 0)
    v.far[place] = v.fas[place]
    back_spec = jnp.dot(v.qb[...], g_coeffs.astype(bf16), preferred_element_type=f32)
    v.s6[...] = back_spec.astype(bf16).reshape(n.nb, piece, LANES)
    exchange("a6", "lat", me_b, n.nb, v.s6, v.r6)
    r_c(1)

    arrived("glo", v.ghalo.at[0])
    arrived("ghi", v.ghalo.at[1])
    spread(0, v.ghalo[0, 0])
    spread(1, v.ghalo[0, 1])

    arrived("fa", v.far.at[pl.ds(0, 2 * n.nx - 1)])
    v.fbs[...] = jnp.sum(v.far[...].astype(f32), axis=0).astype(bf16)

    def send_fb(t, carry):
        z = lax.rem(me_z + t, n.nz)
        copy("fb", v.fbs, v.fbr.at[me_z], {"lat": z * n.nx + me_x}).start()
        return carry

    lax.fori_loop(1, n.nz, send_fb, 0)
    v.fbr[me_z] = v.fbs[...]
    r_c(2)
    r_d(0)

    spread(HALO + n.rows, v.ghalo[1, 0])
    spread(HALO + n.rows + 1, v.ghalo[1, 1])
    r_d(1)

    arrived("a6", v.r6.at[pl.ds(0, n.nb - 1)])
    for r, row in enumerate(from_pieces(v.fwd, v.r6)):
        base = jnp.concatenate([v.cot8[2 * r], v.cot8[2 * r + 1]], axis=1).astype(f32)
        v.wide[:, r, :] = base + row + v.back[r]
    v.gfield[...] = v.wide[...].astype(bf16)

    arrived("fb", v.fbr.at[pl.ds(0, n.nz - 1)])
    ftot = jnp.sum(v.fbr[...].astype(f32), axis=0)
    v.fcr[place] = ftot

    def send_fc(t, carry):
        p, to = near(t)
        copy("fc", v.fcr.at[place], v.fcr.at[place], to).start()
        return carry

    lax.fori_loop(1, 2 * n.nx, send_fc, 0)
    v.gdw[...] = pltpu.roll(ftot, 64, 1)[: n.ks, : n.cl] * n.scale

    r_d(2)
    for k in range(n.kc):
        r_e(k)
    copy("re", v.wtot.at[me_e], v.wtot.at[me_e], {"ens": 1 - me_e}).start()

    arrived("fc", v.fcr.at[pl.ds(0, 2 * n.nx - 1)])
    flipped = jnp.transpose(v.fcr[...].reshape(2 * n.deg, LANES))
    for t in range(2):
        v.gsw[t] = flipped[: n.cl, t * n.deg : (t + 1) * n.deg]

    arrived("re", v.wtot.at[0])
    for k in range(n.kc):
        lanes = slice(k * LANES, (k + 1) * LANES)
        upper = slice(n.chans + k * LANES, n.chans + (k + 1) * LANES)
        low = n.slot // 2
        v.gh[:, lanes] = v.wtot[0, k, :share, :] * n.scale
        v.gh[:, upper] = v.wtot[0, k, low : low + share, :] * n.scale
        v.go[:, lanes] = v.wtot[1, k, : 2 * share, :] * n.scale

    for phase, ref in (("a1", v.s1), ("a2", v.s2), ("a5", v.s5), ("a6", v.s6)):
        left(phase, ref.at[pl.ds(0, n.nb - 1)])
    for phase, ref in (("cot", v.cot8), ("mix", v.mixs), ("grd", v.gs)):
        left(phase, ref.at[pl.ds(0, n.ng - 1)])
    left("hi", v.halo.at[1])
    left("lo", v.halo.at[0])
    left("ghi", v.ghalo.at[1])
    left("glo", v.ghalo.at[0])
    for k in range(n.kc):
        left(f"ra{k}", v.war.at[k])
        left(f"rb{k}", v.wbs.at[k, pl.ds(0, n.nx - 1)])
        left(f"rc{k}", v.wcs.at[k, pl.ds(0, n.nz - 1)])
        left(f"rd{k}", v.wdr.at[k, pl.ds(0, n.ng - 1)])
    left("re", v.wtot.at[0])
    left("fa", v.fas.at[pl.ds(0, 2 * n.nx - 1)])
    left("fb", v.fbr.at[pl.ds(0, n.nz - 1)])
    left("fc", v.fcr.at[pl.ds(0, 2 * n.nx - 1)])


class Sizes:
    pass


def copies(*refs):
    count = len(refs) // 2
    for source, target in zip(refs[:count], refs[count:]):
        target[...] = source[...]


def shards(
    nx,
    field,
    cotangent,
    spec_weight,
    disco_coef,
    disco_weight,
    disco_rows,
    disco_shift,
    w_hidden,
    w_output,
):
    n = Sizes()
    _, n.cl, n.rows, n.lon = field.shape
    n.ne, n.nb, n.ng = (lax.axis_size(a) for a in ("ens", "lat", "chan"))
    n.nx = nx
    n.nz = n.nb // nx
    n.lat = n.rows * n.nb
    n.modes = n.lat // 2
    n.ml = n.modes // n.nb
    n.qn = 2 * n.ml
    n.deg = spec_weight.shape[1]
    n.ks = disco_coef.shape[1]
    n.chans, n.hid = w_hidden.shape
    n.frows = n.deg // n.nx
    n.kc = n.chans // LANES
    n.slot = 2 * (-(-(n.chans // n.nb) // 16) * 16)
    n.scale = 1.0 / math.sqrt(n.ne * n.lat * n.lon)
    plain, weighted, forward, inverse = constant_tables(n.lat, n.lon, n.modes, n.deg, n.nb)
    scratches = scratch(n)
    vmem = pl.BlockSpec(memory_space=pltpu.VMEM)
    smem = pl.BlockSpec(memory_space=pltpu.SMEM)
    hbm = pl.BlockSpec(memory_space=pl.ANY)
    share = n.chans // n.nb
    shapes = (
        jax.ShapeDtypeStruct((n.cl, n.rows, n.lon), bf16),
        jax.ShapeDtypeStruct((2, n.cl, n.deg), f32),
        jax.ShapeDtypeStruct((n.ks, n.cl), f32),
        jax.ShapeDtypeStruct((share, n.hid), f32),
        jax.ShapeDtypeStruct((2 * share, n.chans), f32),
    )
    results = pl.pallas_call(
        functools.partial(kernel, n, ARGS + tuple(scratches)),
        out_shape=shapes,
        in_specs=[vmem] * 8 + [smem] * 3 + [hbm] * 2,
        out_specs=(vmem,) * 5,
        scratch_shapes=list(scratches.values()),
        compiler_params=pltpu.CompilerParams(
            collective_id=0, has_side_effects=True, vmem_limit_bytes=56 * 1024 * 1024
        ),
    )(
        field[0],
        cotangent[0],
        jnp.transpose(spec_weight, (0, 2, 1)),
        disco_weight,
        w_hidden,
        w_output,
        jnp.asarray(forward),
        jnp.asarray(inverse),
        jnp.transpose(disco_coef),
        jnp.transpose(disco_rows),
        jnp.transpose(disco_shift),
        jnp.asarray(plain),
        jnp.asarray(weighted),
    )
    grad_field, grad_spec, grad_disco, grad_hidden, grad_output = pl.pallas_call(
        copies,
        out_shape=shapes,
        in_specs=[vmem] * len(shapes),
        out_specs=(vmem,) * len(shapes),
    )(*results)
    return (
        grad_field[None],
        jnp.transpose(grad_spec, (0, 2, 1)),
        grad_disco,
        grad_hidden,
        grad_output,
    )


def solution(mesh, nx=4):
    in_specs = (
        P("ens", "chan", "lat", None),
        P("ens", "chan", "lat", None),
        P(None, None, "chan"),
        P(),
        P(None, "chan"),
        P(),
        P(),
        P(),
        P(),
    )
    out_specs = (
        P("ens", "chan", "lat", None),
        P(None, None, "chan"),
        P(None, "chan"),
        P("lat", None),
        P("lat", None),
    )
    return jax.shard_map(
        functools.partial(shards, nx),
        mesh=mesh,
        in_specs=in_specs,
        out_specs=out_specs,
        check_vma=False,
    )
```

```python
import functools
import math

import jax
import jax.numpy as jnp
import ml_dtypes
import numpy as np
from jax import lax
from jax.experimental import pallas as pl
from jax.experimental.pallas import tpu as pltpu
from jax.sharding import PartitionSpec as P

MESH = pl.DeviceIdType.MESH
HALO = 2
LANES = 128
norm_eps = 1e-06
inv_root_two = 0.7071067811865476
inv_root_tau = 0.3989422804014327
f32 = jnp.float32
bf16 = jnp.bfloat16
NT = (((1,), (1,)), ((), ()))


def legendre_table(lat_count, order_count, degree_count):
    theta = math.pi * (np.arange(lat_count) + 0.5) / lat_count
    cosine, sine = np.cos(theta), np.sin(theta)
    table = np.zeros((order_count, degree_count, lat_count))
    for m in range(order_count):
        start = 0.5 * (
            math.log((2 * m + 1) / (4 * math.pi))
            + math.lgamma(m + 0.5)
            - math.lgamma(m + 1)
            - math.lgamma(0.5)
        )
        if m < degree_count:
            table[m, m] = np.exp(start + m * np.log(sine))
        for l in range(m + 1, degree_count):
            a = math.sqrt((4 * l * l - 1) / (l * l - m * m))
            b = math.sqrt(((l - 1) ** 2 - m * m) / (4 * (l - 1) ** 2 - 1))
            before = table[m, l - 2] if l >= 2 else 0.0
            table[m, l] = a * (cosine * table[m, l - 1] - b * before)
    return table


def constant_tables(lat_count, lon_count, mode_count, degree_count, bands):
    legendre = legendre_table(lat_count, mode_count, degree_count)
    sine = np.sin(math.pi * (np.arange(lat_count) + 0.5) / lat_count)
    quadrature = (2 * math.pi / lon_count) * (math.pi / lat_count) * sine
    here = mode_count // bands
    shape = (bands, here * degree_count, lat_count)
    plain = legendre.reshape(shape).astype(np.float32).astype(ml_dtypes.bfloat16)
    weighted = (legendre * quadrature).reshape(shape).astype(np.float32).astype(ml_dtypes.bfloat16)
    modes = np.arange(mode_count)
    phase = 2 * math.pi * ((modes[:, None] * np.arange(lon_count)[None, :]) % lon_count) / lon_count
    scale = np.where(modes == 0, 1.0, 2.0)[:, None]
    cos_rows = np.cos(phase).reshape(bands, 1, here, lon_count)
    sin_rows = -np.sin(phase).reshape(bands, 1, here, lon_count)
    forward = np.concatenate([cos_rows, sin_rows], axis=1).reshape(2 * mode_count, lon_count)
    doubled = np.repeat(scale.reshape(bands, 1, here, 1), 2, axis=1).reshape(2 * mode_count, 1)
    cast = lambda v: v.astype(np.float32).astype(ml_dtypes.bfloat16)
    return plain, weighted, cast(forward), cast(forward * doubled)


class Names:
    def __init__(self, names, refs):
        for name, ref in zip(names, refs, strict=True):
            setattr(self, name, ref)


ARGS = (
    "field", "cot", "sw", "dw", "wh", "wo", "fwd", "inv", "coef", "rows", "shift", "p_hbm",
    "q_hbm", "gfield", "gsw", "gdw", "gh", "go",
)
DMAS = (
    "a1", "a2", "cot", "mix", "grd", "a5", "a6", "lo", "hi", "glo", "ghi", "re", "fa", "fb", "fc",
    "ra0", "ra1", "ra2", "rb0", "rb1", "rb2", "rc0", "rc1", "rc2", "rd0", "rd1", "rd2",
)
S = {name: i for i, name in enumerate(DMAS)}


def scratch(n):
    piece = n.qn * n.rows
    return dict(
        pt=pltpu.VMEM((n.ml * n.deg, n.lat), bf16),
        qt=pltpu.VMEM((n.ml * n.deg, n.lat), bf16),
        qa=pltpu.VMEM((n.qn * n.deg, n.nb * piece), bf16),
        pa=pltpu.VMEM((n.qn * n.deg, n.nb * piece), bf16),
        qb=pltpu.VMEM((n.nb * piece, n.qn * n.deg), bf16),
        pb=pltpu.VMEM((n.nb * piece, n.qn * n.deg), bf16),
        wht=pltpu.VMEM((n.hid, n.chans), bf16),
        spread_rows=pltpu.VMEM((n.nb * piece, LANES), f32),
        s1=pltpu.VMEM((n.nb, piece, LANES), bf16),
        r1=pltpu.VMEM((n.nb, piece, LANES), bf16),
        s2=pltpu.VMEM((n.nb, piece, LANES), bf16),
        r2=pltpu.VMEM((n.nb, piece, LANES), bf16),
        s5=pltpu.VMEM((n.nb, piece, LANES), bf16),
        r5=pltpu.VMEM((n.nb, piece, LANES), bf16),
        s6=pltpu.VMEM((n.nb, piece, LANES), bf16),
        r6=pltpu.VMEM((n.nb, piece, LANES), bf16),
        coeffs=pltpu.VMEM((n.qn * n.deg, LANES), f32),
        sww=pltpu.VMEM((2, n.ml * n.deg, LANES), f32),
        halo=pltpu.VMEM((2, HALO, n.cl, n.lon), bf16),
        ghalo=pltpu.VMEM((2, HALO, n.cl, n.lon), bf16),
        fext=pltpu.VMEM((n.rows + 2 * HALO, n.cl, n.lon), f32),
        gm=pltpu.VMEM((n.rows, n.cl, n.lon), bf16),
        shifted=pltpu.VMEM((n.rows * n.ks, n.cl, n.lon), f32),
        square=pltpu.VMEM((LANES, LANES), f32),
        wcol=pltpu.VMEM((n.ks, n.cl, n.lon), f32),
        disco=pltpu.VMEM((n.rows, n.cl, n.lon), f32),
        back=pltpu.VMEM((n.rows, n.cl, n.lon), f32),
        dgrad=pltpu.VMEM((LANES, LANES), f32),
        cotall=pltpu.VMEM((n.ng, n.cl, LANES), bf16),
        mixs=pltpu.VMEM((n.ng, n.cl, LANES), bf16),
        mixall=pltpu.VMEM((n.ng, n.cl, LANES), bf16),
        gact=pltpu.VMEM((n.hid, LANES), f32),
        gpre=pltpu.VMEM((n.hid, LANES), bf16),
        gs=pltpu.VMEM((n.ng, n.cl, LANES), bf16),
        gr=pltpu.VMEM((n.ng, n.cl, LANES), bf16),
        wide=pltpu.VMEM((n.cl, n.rows, n.lon), f32),
        fld=pltpu.VMEM((n.rows, n.cl, n.lon), bf16),
        cot8=pltpu.VMEM((n.ng, n.cl, LANES), bf16),
        n32=pltpu.VMEM((n.chans, LANES), f32),
        np32=pltpu.VMEM((n.chans, LANES), f32),
        ap32=pltpu.VMEM((n.hid, LANES), f32),
        was=pltpu.VMEM((2, n.kc - 1, n.nx, n.hid // n.nx, LANES), bf16),
        war=pltpu.VMEM((n.kc - 1, n.nx, n.hid // n.nx, LANES), bf16),
        wbs=pltpu.VMEM((n.kc - 1, n.nx, n.hid // n.nx, LANES), bf16),
        wbr=pltpu.VMEM((n.kc - 1, n.nx, n.hid // n.nx, LANES), bf16),
        zas=pltpu.VMEM((2, n.nz, n.hid // n.nz, LANES), bf16),
        zar=pltpu.VMEM((n.nz, n.hid // n.nz, LANES), bf16),
        zbs=pltpu.VMEM((n.nz, n.hid // n.nz, LANES), bf16),
        zbr=pltpu.VMEM((n.nz, n.hid // n.nz, LANES), bf16),
        wsum=pltpu.VMEM((n.hid // n.nx, LANES), f32),
        wslot=pltpu.VMEM((n.nz, n.slot, LANES), f32),
        wcs=pltpu.VMEM((n.kc, n.nz, n.slot, LANES), bf16),
        wcr=pltpu.VMEM((n.kc, n.nz, n.slot, LANES), bf16),
        wds=pltpu.VMEM((n.kc, n.slot, LANES), bf16),
        wdr=pltpu.VMEM((n.kc, n.ng, n.slot, LANES), bf16),
        wtot=pltpu.VMEM((2, n.kc, n.slot, LANES), f32),
        fas=pltpu.VMEM((2 * n.nx, n.frows, LANES), bf16),
        far=pltpu.VMEM((2 * n.nx, n.frows, LANES), bf16),
        fbs=pltpu.VMEM((n.frows, LANES), bf16),
        fbr=pltpu.VMEM((n.nz, n.frows, LANES), bf16),
        fcr=pltpu.VMEM((2 * n.nx, n.frows, LANES), f32),
        load_sem=pltpu.SemaphoreType.DMA((2,)),
        send=pltpu.SemaphoreType.DMA((len(DMAS),)),
        recv=pltpu.SemaphoreType.DMA((len(DMAS),)),
    )


def kernel(n, names, *refs):
    v = Names(list(names), refs)
    me_e, me_b, me_g = (lax.axis_index(a) for a in ("ens", "lat", "chan"))
    me_z, me_x = lax.div(me_b, n.nx), lax.rem(me_b, n.nx)
    first = me_b * n.rows
    piece = n.qn * n.rows
    total_rows = n.nb * piece

    def copy(phase, src, dst, device):
        return pltpu.make_async_remote_copy(
            src_ref=src,
            dst_ref=dst,
            send_sem=v.send.at[S[phase]],
            recv_sem=v.recv.at[S[phase]],
            device_id=device,
            device_id_type=MESH,
        )

    def arrived(phase, ref):
        pltpu.make_async_copy(ref, ref, v.recv.at[S[phase]]).wait()

    def left(phase, ref):
        pltpu.make_async_copy(ref, ref, v.send.at[S[phase]]).wait()

    def lat_peer(k):
        return lax.rem(me_b + k, n.nb)

    def farthest_first(t, count):
        return count // 2 + jnp.where(lax.rem(t, 2) == 0, -lax.div(t, 2), lax.div(t + 1, 2))

    def lat_at(t):
        u = lax.div(t, n.nx)
        far = n.nz // 2
        dz = jnp.where(lax.rem(u, 2) == 0, far - lax.div(u, 2), far + lax.div(u + 1, 2))
        dx = lax.rem(n.nx // 2 + n.nx - lax.rem(t, n.nx), n.nx)
        dx = jnp.where(u == n.nz - 1, n.nx // 2 + lax.rem(t, n.nx) - 1, dx)
        return lax.rem(me_z + n.nz + dz, n.nz) * n.nx + lax.rem(me_x + n.nx + dx, n.nx)

    def exchange(phase, axis, me, count, src, dst, whole=False):
        def step(k, carry):
            d = lax.rem(me + farthest_first(k, count), count)
            copy(phase, src if whole else src.at[d], dst.at[me], {axis: d}).start()
            return carry

        def to_lat(t, carry):
            d = lat_at(t)
            copy(phase, src.at[d], dst.at[me], {axis: d}).start()
            return carry

        if axis == "lat":
            lax.fori_loop(0, count - 1, to_lat, 0, unroll=True)
        else:
            lax.fori_loop(0, count - 1, step, 0)
        dst[me] = src[...] if whole else src[me]

    barrier = pltpu.get_barrier_semaphore()

    def greet(device):
        pl.semaphore_signal(barrier, inc=1, device_id=device, device_id_type=MESH)

    def greet_lat(k, carry):
        greet({"lat": lat_at(k)})
        return carry

    def greet_chan(k, carry):
        greet({"chan": lax.rem(me_g + k, n.ng)})
        return carry

    def greet_ens(k, carry):
        greet({"ens": 1 - me_e, "lat": me_z * n.nx + k})
        return carry

    lax.fori_loop(0, n.nb - 1, greet_lat, 0)
    lax.fori_loop(1, n.ng, greet_chan, 0)
    lax.fori_loop(0, n.nx, greet_ens, 0)

    load_p = pltpu.make_async_copy(v.p_hbm.at[me_b], v.pt, v.load_sem.at[0])
    load_q = pltpu.make_async_copy(v.q_hbm.at[me_b], v.qt, v.load_sem.at[1])
    load_p.start()
    load_q.start()

    def to_pieces(table, row_of, out):
        for r in range(n.rows):
            part = lax.dot_general(table[...], row_of(r), NT, preferred_element_type=f32)
            v.spread_rows[pl.ds(r, 2 * n.modes, stride=n.rows), :] = jnp.concatenate(
                [part, jnp.zeros((2 * n.modes, LANES - n.cl), f32)], axis=1
            )
        out[...] = v.spread_rows[...].astype(bf16).reshape(n.nb, piece, LANES)

    def from_pieces(table, pieces):
        v.spread_rows[...] = pieces[...].reshape(total_rows, LANES).astype(f32)
        rows = []
        for r in range(n.rows):
            part = v.spread_rows[pl.ds(r, 2 * n.modes, stride=n.rows), :]
            flipped = jnp.transpose(part).astype(bf16)[: n.cl]
            rows.append(jnp.dot(flipped, table[...], preferred_element_type=f32))
        return rows

    v.wide[...] = v.field[...].astype(f32)
    for r in range(n.rows):
        row = v.wide[:, r, :]
        v.fext[HALO + r] = row
        v.fld[r] = row.astype(bf16)
    to_pieces(v.fwd, lambda r: v.fld[r], v.s1)
    v.wide[...] = v.cot[...].astype(f32)
    for r in range(n.rows):
        row = v.wide[:, r, :].astype(bf16)
        v.cot8[2 * r] = row[:, :LANES]
        v.cot8[2 * r + 1] = row[:, LANES:]
    pl.semaphore_wait(barrier, n.nb - 1 + n.ng - 1 + n.nx)

    exchange("a1", "lat", me_b, n.nb, v.s1, v.r1)
    below, above = lat_peer(n.nb - 1), lat_peer(1)
    top, bottom = pl.ds(0, HALO), pl.ds(n.rows - HALO, HALO)
    copy("hi", v.fld.at[top], v.halo.at[1], {"lat": below}).start()
    copy("lo", v.fld.at[bottom], v.halo.at[0], {"lat": above}).start()
    exchange("cot", "chan", me_g, n.ng, v.cot8, v.cotall)

    load_p.wait()
    load_q.wait()

    half = n.ml * n.deg
    wide = (n.lat, total_rows)
    column = lax.broadcasted_iota(jnp.int32, wide, 1)
    row_id = lax.broadcasted_iota(jnp.int32, wide, 0)
    lat_of = lax.div(column, piece) * n.rows + lax.rem(column, n.rows)
    expand = jnp.where(lat_of == row_id, 1.0, 0.0).astype(bf16)
    q_of = lax.div(lax.rem(lax.broadcasted_iota(jnp.int32, (half, total_rows), 1), piece), n.rows)
    ml_of = lax.div(lax.broadcasted_iota(jnp.int32, (half, total_rows), 0), n.deg)

    def expanded(table, out):
        both = jnp.dot(table[...], expand, preferred_element_type=f32)
        for t in range(2):
            keep = q_of == ml_of + t * n.ml
            out[t * half : (t + 1) * half, :] = jnp.where(keep, both, 0.0).astype(bf16)

    expanded(v.qt, v.qa)
    expanded(v.pt, v.pa)
    for t in range(2):
        mine = slice(t * half, (t + 1) * half)
        v.pb[:, mine] = jnp.transpose(v.pa[mine, :].astype(f32)).astype(bf16)
    v.square[...] = jnp.zeros((LANES, LANES), f32)
    for t in range(2):
        v.square[: n.cl, : n.deg] = v.sw[t]
        block = jnp.transpose(v.square[...])[: n.deg]
        for m in range(n.ml):
            v.sww[t, m * n.deg : (m + 1) * n.deg, :] = block

    arrived("a1", v.r1.at[pl.ds(0, n.nb - 1)])
    spectrum = v.r1[...].reshape(total_rows, LANES)
    coeffs = jnp.dot(v.qa[...], spectrum, preferred_element_type=f32)
    v.coeffs[...] = coeffs
    real, imag = coeffs[:half], coeffs[half:]
    s0, s1 = v.sww[0], v.sww[1]
    filtered = jnp.concatenate([s0 * real - s1 * imag, s0 * imag + s1 * real], axis=0)
    synth = jnp.dot(v.pb[...], filtered.astype(bf16), preferred_element_type=f32)
    v.s2[...] = synth.astype(bf16).reshape(n.nb, piece, LANES)
    exchange("a2", "lat", me_b, n.nb, v.s2, v.r2)

    v.square[...] = jnp.zeros((LANES, LANES), f32)
    v.square[: n.ks, : n.cl] = v.dw[...]
    columns = jnp.transpose(v.square[...])
    for k in range(n.ks):
        v.wcol[k] = jnp.broadcast_to(columns[: n.cl, k : k + 1], (n.cl, n.lon))
    arrived("lo", v.halo.at[0])
    arrived("hi", v.halo.at[1])
    for r in range(HALO):
        v.fext[r] = v.halo[0, r].astype(f32)
        v.fext[HALO + n.rows + r] = v.halo[1, r].astype(f32)

    for r in range(n.rows):

        def tap(k, total, r=r):
            source = v.rows[k, first + r] - first + HALO
            source = jnp.minimum(jnp.maximum(source, 0), n.rows + 2 * HALO - 1)
            amount = lax.rem(n.lon - v.shift[k, first + r], n.lon)
            moved = pltpu.roll(v.fext[source], amount, 1)
            v.shifted[r * n.ks + k] = moved
            return total + (v.coef[k, first + r] * v.wcol[k]) * moved

        v.disco[r] = lax.fori_loop(0, n.ks, tap, jnp.zeros((n.cl, n.lon), f32), unroll=True)

    for t in range(2):
        mine = slice(t * half, (t + 1) * half)
        v.qb[:, mine] = jnp.transpose(v.qa[mine, :].astype(f32)).astype(bf16)
    v.wht[...] = jnp.transpose(v.wh[...].astype(f32)).astype(bf16)
    arrived("cot", v.cotall.at[pl.ds(0, n.ng - 1)])
    v.gact[...] = jnp.dot(
        v.wo[...], v.cotall[...].reshape(n.chans, LANES), preferred_element_type=f32
    )

    arrived("a2", v.r2.at[pl.ds(0, n.nb - 1)])
    for r, row in enumerate(from_pieces(v.inv, v.r2)):
        mixed = (row + v.disco[r]).astype(bf16)
        v.mixs[2 * r] = mixed[:, :LANES]
        v.mixs[2 * r + 1] = mixed[:, LANES:]
    exchange("mix", "chan", me_g, n.ng, v.mixs, v.mixall)

    arrived("mix", v.mixall.at[pl.ds(0, n.ng - 1)])
    mixed = v.mixall[...].reshape(n.chans, LANES).astype(f32)
    rscale = lax.rsqrt(jnp.sum(mixed * mixed, axis=0, keepdims=True) * (1.0 / n.chans) + norm_eps)
    normed32 = mixed * rscale
    normed = normed32.astype(bf16)
    v.n32[...] = normed32
    preact = jnp.dot(v.wht[...], normed, preferred_element_type=f32)
    cumulative = 0.5 * (1.0 + lax.erf(preact * inv_root_two))
    density = jnp.exp(-0.5 * preact * preact) * inv_root_tau
    activated = preact * cumulative
    grad_pre = (v.gact[...] * (cumulative + preact * density)).astype(bf16)
    v.gpre[...] = grad_pre
    grad_normed = jnp.dot(v.wh[...], grad_pre, preferred_element_type=f32)
    along = jnp.sum(grad_normed * normed32, axis=0, keepdims=True) * (1.0 / n.chans)
    grad_mixed = (rscale * (grad_normed - normed32 * along)).astype(bf16)
    v.gs[...] = grad_mixed.reshape(n.ng, n.cl, LANES)
    exchange("grd", "chan", me_g, n.ng, v.gs, v.gr)

    share = n.chans // n.nb
    for x in range(n.nx):
        for z in range(n.nz):
            at, to = (z * n.nx + x) * share, (x * n.nz + z) * share
            v.np32[to : to + share, :] = v.n32[at : at + share, :]
            v.ap32[2 * to : 2 * (to + share), :] = activated[2 * at : 2 * (at + share)]
    plain = (v.n32[...].astype(bf16), activated.astype(bf16))
    sorted_rows = (v.np32[...].astype(bf16), v.ap32[...].astype(bf16))
    adjoint = v.cotall[...].reshape(n.chans, LANES)
    last = n.kc - 1

    def path(k):
        along_x = (n.nx, me_x, lambda x: {"lat": me_z * n.nx + x})
        along_z = (n.nz, me_z, lambda z: {"lat": z * n.nx + me_x})
        return (along_z, along_x) if k == last else (along_x, along_z)

    def first_refs(k):
        if k == last:
            return v.zas, v.zar, v.zbs, v.zbr
        return v.was.at[:, k], v.war.at[k], v.wbs.at[k], v.wbr.at[k]

    def r_a(k):
        count = path(k)[0][0]
        cols, depth = n.chans // count, n.hid // count
        normed, active = plain if k == last else sorted_rows
        mine, other, _, _ = first_refs(k)
        for half in range(2):
            at = half * n.chans + k * LANES
            hidden = lax.dot_general(
                normed, v.gpre[at : at + LANES, :], NT, preferred_element_type=f32
            ).astype(bf16)
            for p in range(count):
                rows = hidden[p * cols : (p + 1) * cols]
                mine[0, p, half * cols : (half + 1) * cols, :] = rows
        output = lax.dot_general(
            active, adjoint[k * LANES : (k + 1) * LANES], NT, preferred_element_type=f32
        )
        mine[1] = output.astype(bf16).reshape(count, depth, LANES)
        copy(f"ra{k}", mine.at[1 - me_e], other, {"ens": 1 - me_e}).start()

    def r_b(k):
        count, place, device = path(k)[0]
        mine, other, out, into = first_refs(k)
        arrived(f"ra{k}", other)
        out[...] = (mine[me_e].astype(f32) + other[...].astype(f32)).astype(bf16)

        def send(t, carry):
            p = lax.rem(place + farthest_first(t, count), count)
            copy(f"rb{k}", out.at[p], into.at[place], device(p)).start()
            return carry

        lax.fori_loop(0, count - 1, send, 0)
        into[place] = out[place]

    def r_c(k):
        (count, _, _), (owners, place, device) = path(k)
        into = first_refs(k)[3]
        cols, depth = n.chans // count, n.hid // count
        arrived(f"rb{k}", into.at[pl.ds(0, count - 1)])
        v.wsum[:depth, :] = jnp.sum(into[...].astype(f32), axis=0)

        @pl.when(me_e == 0)
        def _():
            for p in range(owners):
                for half in range(2):
                    at, to = half * cols + p * share, half * (n.slot // 2)
                    v.wslot[p, to : to + share, :] = v.wsum[at : at + share, :]

        @pl.when(me_e == 1)
        def _():
            for p in range(owners):
                v.wslot[p, : 2 * share, :] = v.wsum[2 * p * share : 2 * (p + 1) * share, :]

        v.wcs[k, :owners] = v.wslot[:owners].astype(bf16)

        def send(t, carry):
            p = lax.rem(place + farthest_first(t, owners), owners)
            copy(f"rc{k}", v.wcs.at[k, p], v.wcr.at[k, place], device(p)).start()
            return carry

        lax.fori_loop(0, owners - 1, send, 0)
        v.wcr[k, place] = v.wcs[k, place]

    def r_d(k):
        owners = path(k)[1][0]
        arrived(f"rc{k}", v.wcr.at[k, pl.ds(0, owners - 1)])
        v.wds[k] = jnp.sum(v.wcr[k, :owners].astype(f32), axis=0).astype(bf16)

        def send(t, carry):
            g = lax.rem(me_g + t, n.ng)
            copy(f"rd{k}", v.wds.at[k], v.wdr.at[k, me_g], {"chan": g}).start()
            return carry

        lax.fori_loop(1, n.ng, send, 0)
        v.wdr[k, me_g] = v.wds[k]

    def r_e(k):
        arrived(f"rd{k}", v.wdr.at[k, pl.ds(0, n.ng - 1)])
        v.wtot[me_e, k] = jnp.sum(v.wdr[k].astype(f32), axis=0)

    for k in range(n.kc):
        r_a(k)
    r_b(0)

    arrived("grd", v.gr.at[pl.ds(0, n.ng - 1)])
    for r in range(n.rows):
        v.gm[r] = jnp.concatenate([v.gr[2 * r], v.gr[2 * r + 1]], axis=1)
    to_pieces(v.inv, lambda r: v.gm[r], v.s5)
    exchange("a5", "lat", me_b, n.nb, v.s5, v.r5)
    copy("ghi", v.gm.at[top], v.ghalo.at[1], {"lat": below}).start()
    copy("glo", v.gm.at[bottom], v.ghalo.at[0], {"lat": above}).start()
    r_b(1)
    r_b(2)

    lane = lax.broadcasted_iota(jnp.int32, (n.cl, LANES), 1)

    def weight_tap(k, total):
        inner = jnp.zeros((n.cl, n.lon), f32)
        for r in range(n.rows):
            inner = inner + v.coef[k, first + r] * (
                v.shifted[r * n.ks + k] * v.gm[r].astype(f32)
            )
        return total + jnp.where(lane == k, jnp.sum(inner, axis=1, keepdims=True), 0.0)

    weight_grad = lax.fori_loop(
        0, n.ks, weight_tap, jnp.zeros((n.cl, LANES), f32), unroll=True
    )
    v.square[...] = jnp.zeros((LANES, LANES), f32)
    v.square[: n.cl, :] = weight_grad
    v.dgrad[...] = jnp.transpose(v.square[...])

    for r in range(n.rows):
        v.back[r] = jnp.zeros((n.cl, n.lon), f32)

    def spread(at, rows_of):
        values = rows_of.astype(f32)
        wanted = first - HALO + at
        held = jnp.minimum(jnp.maximum(wanted, 0), n.lat - 1)
        real_row = jnp.where(held == wanted, 1.0, 0.0).astype(f32)
        targets = [r for r in range(n.rows) if abs(at - HALO - r) <= HALO]

        def tap(k, totals):
            moved = pltpu.roll(values, lax.rem(n.lon + v.shift[k, held], n.lon), 1) * v.wcol[k]
            factor = v.coef[k, held] * real_row
            to = v.rows[k, held]
            return tuple(
                total + jnp.where(to == first + r, factor, 0.0) * moved
                for r, total in zip(targets, totals)
            )

        start = tuple(v.back[r] for r in targets)
        for r, total in zip(targets, lax.fori_loop(0, n.ks, tap, start, unroll=True)):
            v.back[r] = total

    for r in range(n.rows):
        if r == n.rows // 2:
            r_c(0)
        spread(HALO + r, v.gm[r])

    arrived("a5", v.r5.at[pl.ds(0, n.nb - 1)])
    grads = jnp.dot(v.pa[...], v.r5[...].reshape(total_rows, LANES), preferred_element_type=f32)
    g_real, g_imag = grads[:half], grads[half:]
    s0, s1 = v.sww[0], v.sww[1]
    g_coeffs = jnp.concatenate([s0 * g_real + s1 * g_imag, s0 * g_imag - s1 * g_real], axis=0)
    real, imag = v.coeffs[:half, :], v.coeffs[half:, :]
    terms = (g_real * real + g_imag * imag, g_imag * real - g_real * imag)
    disco_part = pltpu.roll(v.dgrad[: n.frows, :], 64, 1)
    low_lanes = lax.broadcasted_iota(jnp.int32, (n.frows, LANES), 1) < 64
    for t in range(2):
        part = terms[t][: n.deg]
        for m in range(1, n.ml):
            part = part + terms[t][m * n.deg : (m + 1) * n.deg]
        for x in range(n.nx):
            rows = part[x * n.frows : (x + 1) * n.frows]
            v.fas[t * n.nx + x] = jnp.where(low_lanes, rows, disco_part).astype(bf16)
    place = me_e * n.nx + me_x

    def near(t):
        p = lax.rem(place + t, 2 * n.nx)
        return p, {"ens": lax.div(p, n.nx), "lat": me_z * n.nx + lax.rem(p, n.nx)}

    def send_fa(t, carry):
        p, to = near(t)
        copy("fa", v.fas.at[p], v.far.at[place], to).start()
        return carry

    lax.fori_loop(1, 2 * n.nx, send_fa, 0)
    v.far[place] = v.fas[place]
    back_spec = jnp.dot(v.qb[...], g_coeffs.astype(bf16), preferred_element_type=f32)
    v.s6[...] = back_spec.astype(bf16).reshape(n.nb, piece, LANES)
    exchange("a6", "lat", me_b, n.nb, v.s6, v.r6)
    r_c(1)

    arrived("glo", v.ghalo.at[0])
    arrived("ghi", v.ghalo.at[1])
    spread(0, v.ghalo[0, 0])
    spread(1, v.ghalo[0, 1])

    r_c(2)
    arrived("fa", v.far.at[pl.ds(0, 2 * n.nx - 1)])
    v.fbs[...] = jnp.sum(v.far[...].astype(f32), axis=0).astype(bf16)

    def send_fb(t, carry):
        z = lax.rem(me_z + t, n.nz)
        copy("fb", v.fbs, v.fbr.at[me_z], {"lat": z * n.nx + me_x}).start()
        return carry

    lax.fori_loop(1, n.nz, send_fb, 0)
    v.fbr[me_z] = v.fbs[...]
    r_d(0)

    spread(HALO + n.rows, v.ghalo[1, 0])
    spread(HALO + n.rows + 1, v.ghalo[1, 1])
    r_d(1)

    r_d(2)

    arrived("a6", v.r6.at[pl.ds(0, n.nb - 1)])
    for r, row in enumerate(from_pieces(v.fwd, v.r6)):
        base = jnp.concatenate([v.cot8[2 * r], v.cot8[2 * r + 1]], axis=1).astype(f32)
        v.wide[:, r, :] = base + row + v.back[r]
    v.gfield[...] = v.wide[...].astype(bf16)

    arrived("fb", v.fbr.at[pl.ds(0, n.nz - 1)])
    ftot = jnp.sum(v.fbr[...].astype(f32), axis=0)
    v.fcr[place] = ftot

    def send_fc(t, carry):
        p, to = near(t)
        copy("fc", v.fcr.at[place], v.fcr.at[place], to).start()
        return carry

    lax.fori_loop(1, 2 * n.nx, send_fc, 0)
    v.gdw[...] = pltpu.roll(ftot, 64, 1)[: n.ks, : n.cl] * n.scale

    for k in range(n.kc):
        r_e(k)
    copy("re", v.wtot.at[me_e], v.wtot.at[me_e], {"ens": 1 - me_e}).start()

    arrived("fc", v.fcr.at[pl.ds(0, 2 * n.nx - 1)])
    flipped = jnp.transpose(v.fcr[...].reshape(2 * n.deg, LANES))
    for t in range(2):
        v.gsw[t] = flipped[: n.cl, t * n.deg : (t + 1) * n.deg]

    arrived("re", v.wtot.at[0])
    for k in range(n.kc):
        lanes = slice(k * LANES, (k + 1) * LANES)
        upper = slice(n.chans + k * LANES, n.chans + (k + 1) * LANES)
        low = n.slot // 2
        v.gh[:, lanes] = v.wtot[0, k, :share, :] * n.scale
        v.gh[:, upper] = v.wtot[0, k, low : low + share, :] * n.scale
        v.go[:, lanes] = v.wtot[1, k, : 2 * share, :] * n.scale

    for phase, ref in (("a1", v.s1), ("a2", v.s2), ("a5", v.s5), ("a6", v.s6)):
        left(phase, ref.at[pl.ds(0, n.nb - 1)])
    for phase, ref in (("cot", v.cot8), ("mix", v.mixs), ("grd", v.gs)):
        left(phase, ref.at[pl.ds(0, n.ng - 1)])
    left("hi", v.halo.at[1])
    left("lo", v.halo.at[0])
    left("ghi", v.ghalo.at[1])
    left("glo", v.ghalo.at[0])
    for k in range(n.kc):
        (count, _, _), (owners, _, _) = path(k)
        _, other, out, _ = first_refs(k)
        left(f"ra{k}", other)
        left(f"rb{k}", out.at[pl.ds(0, count - 1)])
        left(f"rc{k}", v.wcs.at[k, pl.ds(0, owners - 1)])
        left(f"rd{k}", v.wdr.at[k, pl.ds(0, n.ng - 1)])
    left("re", v.wtot.at[0])
    left("fa", v.fas.at[pl.ds(0, 2 * n.nx - 1)])
    left("fb", v.fbr.at[pl.ds(0, n.nz - 1)])
    left("fc", v.fcr.at[pl.ds(0, 2 * n.nx - 1)])


class Sizes:
    pass


def copies(*refs):
    count = len(refs) // 2
    for source, target in zip(refs[:count], refs[count:]):
        target[...] = source[...]


def shards(
    nx,
    field,
    cotangent,
    spec_weight,
    disco_coef,
    disco_weight,
    disco_rows,
    disco_shift,
    w_hidden,
    w_output,
):
    n = Sizes()
    _, n.cl, n.rows, n.lon = field.shape
    n.ne, n.nb, n.ng = (lax.axis_size(a) for a in ("ens", "lat", "chan"))
    n.nx = nx
    n.nz = n.nb // nx
    n.lat = n.rows * n.nb
    n.modes = n.lat // 2
    n.ml = n.modes // n.nb
    n.qn = 2 * n.ml
    n.deg = spec_weight.shape[1]
    n.ks = disco_coef.shape[1]
    n.chans, n.hid = w_hidden.shape
    n.frows = n.deg // n.nx
    n.kc = n.chans // LANES
    n.slot = 2 * (-(-(n.chans // n.nb) // 16) * 16)
    n.scale = 1.0 / math.sqrt(n.ne * n.lat * n.lon)
    plain, weighted, forward, inverse = constant_tables(n.lat, n.lon, n.modes, n.deg, n.nb)
    scratches = scratch(n)
    vmem = pl.BlockSpec(memory_space=pltpu.VMEM)
    smem = pl.BlockSpec(memory_space=pltpu.SMEM)
    hbm = pl.BlockSpec(memory_space=pl.ANY)
    share = n.chans // n.nb
    shapes = (
        jax.ShapeDtypeStruct((n.cl, n.rows, n.lon), bf16),
        jax.ShapeDtypeStruct((2, n.cl, n.deg), f32),
        jax.ShapeDtypeStruct((n.ks, n.cl), f32),
        jax.ShapeDtypeStruct((share, n.hid), f32),
        jax.ShapeDtypeStruct((2 * share, n.chans), f32),
    )
    results = pl.pallas_call(
        functools.partial(kernel, n, ARGS + tuple(scratches)),
        out_shape=shapes,
        in_specs=[vmem] * 8 + [smem] * 3 + [hbm] * 2,
        out_specs=(vmem,) * 5,
        scratch_shapes=list(scratches.values()),
        compiler_params=pltpu.CompilerParams(
            collective_id=0, has_side_effects=True, vmem_limit_bytes=56 * 1024 * 1024
        ),
    )(
        field[0],
        cotangent[0],
        jnp.transpose(spec_weight, (0, 2, 1)),
        disco_weight,
        w_hidden,
        w_output,
        jnp.asarray(forward),
        jnp.asarray(inverse),
        jnp.transpose(disco_coef),
        jnp.transpose(disco_rows),
        jnp.transpose(disco_shift),
        jnp.asarray(plain),
        jnp.asarray(weighted),
    )
    grad_field, grad_spec, grad_disco, grad_hidden, grad_output = pl.pallas_call(
        copies,
        out_shape=shapes,
        in_specs=[vmem] * len(shapes),
        out_specs=(vmem,) * len(shapes),
    )(*results)
    return (
        grad_field[None],
        jnp.transpose(grad_spec, (0, 2, 1)),
        grad_disco,
        grad_hidden,
        grad_output,
    )


def solution(mesh, nx=4):
    in_specs = (
        P("ens", "chan", "lat", None),
        P("ens", "chan", "lat", None),
        P(None, None, "chan"),
        P(),
        P(None, "chan"),
        P(),
        P(),
        P(),
        P(),
    )
    out_specs = (
        P("ens", "chan", "lat", None),
        P(None, None, "chan"),
        P(None, "chan"),
        P("lat", None),
        P("lat", None),
    )
    return jax.shard_map(
        functools.partial(shards, nx),
        mesh=mesh,
        in_specs=in_specs,
        out_specs=out_specs,
        check_vma=False,
    )
```
